256 devices in a mesh: dp: 32 (over x, z), tensor: 8 (over y, core).
Axes of the slice: x: 4, y: 4, z: 8, core: 2. Of those that a mesh axis runs over, the one named last changes fastest.
Arguments:
- gate_pre: bfloat16 [16384, 12800], P('dp', 'tensor'), may hold values from -6 to 6
- up_pre: bfloat16 [16384, 12800], P('dp', 'tensor'), may hold values from -6 to 6
- down_codes: bfloat16 [12800, 2560], P(('tensor', 'dp')), may hold values from -127 to 127
- down_scales: float32 [12800, 10], P(('tensor', 'dp')), may hold values from 4e-05 to 0.00024
- cotangent: bfloat16 [16384, 2560], P(('dp', 'tensor')), may hold values from -6 to 6
Outputs:
- layer_out: bfloat16 [16384, 2560], P(('dp', 'tensor'))
- gate_grad: bfloat16 [16384, 12800], P('dp', 'tensor')
- up_grad: bfloat16 [16384, 12800], P('dp', 'tensor')
- weight_grad: float32 [12800, 2560], P(('tensor', 'dp'))
The draws below stay inside these ranges and needn't reach their ends.
All inputs are finite; a program needn't handle non-finite values.
Results may differ from the reference program's by a relative error of at most 0.022.
Values may be sent and summed in bfloat16 or wider, within the bound.
A program may use at most 192 MiB of HBM per device.

```python
import math
import jax
import jax.numpy as jnp
from jax import lax

D = 2560
FF = 12800
BLOCK = 256
TOKENS = 16384
N_DP = 32


def block_levels(key, dims, split, smallest, high):
    factor_of, own = 1.0, jax.random.fold_in(key, 6)
    for dim, blocks in split:
        heights = jnp.exp(jax.random.uniform(jax.random.fold_in(own, dim), (blocks,), jnp.float32, smallest / len(split), high / len(split)))
        factor_of = factor_of * jnp.repeat(heights, dims[dim] // blocks).reshape([-1 if axis == dim else 1 for axis in range(len(dims))])
    return factor_of


def scatter_about(key, shape, scale, limit, shards=(), kind=jnp.bfloat16):
    loudness = block_levels(key, shape, shards, -0.22, 0.18) if shards else 1.0
    values = jax.random.normal(key, shape, jnp.float32) * scale * loudness
    return jnp.minimum(jnp.maximum(values, -limit), limit).astype(kind)


def setup_inputs(seed: int = 0) -> dict:
    seeds = jax.random.split(jax.random.key(seed), 6)
    return {
        "gate_pre": scatter_about(seeds[0], (TOKENS, FF), 1.5, 6.0, ((0, 32), (1, 8))),
        "up_pre": scatter_about(seeds[1], (TOKENS, FF), 1.0, 6.0, ((0, 32), (1, 8))),
        "down_codes": jnp.clip(jax.random.uniform(seeds[2], (FF, D), jnp.float32, -127.0, 127.0) * block_levels(seeds[2], (FF, D), ((0, 256),), -0.4, 0.0), -127.0, 127.0).astype(jnp.bfloat16),
        "down_scales": jnp.clip(jnp.exp(math.log(0.00024) - 1.7917595 * jax.random.uniform(seeds[3], (FF, D // BLOCK), jnp.float32) ** block_levels(seeds[3], (FF, D // BLOCK), ((0, 256),), -0.2, 0.2)), 3.9999998989515007e-05, 0.00024),
        "cotangent": scatter_about(seeds[4], (TOKENS, D), 1.0, 6.0, ((0, 256),)),
    }


def silu_parts(gate_value):
    sigmoid_gate = jax.nn.sigmoid(gate_value)
    return gate_value * sigmoid_gate, sigmoid_gate


def dequantize(code_block, scales):
    row_count, full_width = code_block.shape
    nblocks = scales.shape[1]
    blocks = code_block.astype(jnp.float32).reshape(row_count, nblocks, full_width // nblocks) * scales[:, :, None]
    return blocks.reshape(row_count, full_width).astype(jnp.bfloat16)


def reference(gate_pre, up_pre, down_codes, down_scales, cotangent):
    weight = dequantize(down_codes, down_scales)
    hidden_rows, full_width = weight.shape
    nblocks = down_scales.shape[1]
    group_rows = gate_pre.shape[0] // N_DP

    def group_step(running, pieces):
        gate_piece, up_piece, back_piece = pieces
        gate_value = gate_piece.astype(jnp.float32)
        up_value = up_piece.astype(jnp.float32)
        activated, sigmoid_gate = silu_parts(gate_value)
        hidden = (activated * up_value).astype(jnp.bfloat16)
        layer_rows = jnp.dot(hidden, weight, preferred_element_type=jnp.float32).astype(jnp.bfloat16)
        dhidden = jnp.dot(back_piece, weight.T, preferred_element_type=jnp.float32)
        gate_rows = (dhidden * up_value * sigmoid_gate * (1.0 + gate_value * (1.0 - sigmoid_gate))).astype(jnp.bfloat16)
        up_rows = (dhidden * activated).astype(jnp.bfloat16)
        partial_value = jnp.dot(hidden.T, back_piece, preferred_element_type=jnp.float32)
        blocks = partial_value.reshape(hidden_rows, nblocks, full_width // nblocks)
        scale_rows = (jnp.max(jnp.abs(blocks), axis=2) + 1e-6) / 127.0
        grad_codes = (blocks / scale_rows[:, :, None]).astype(jnp.bfloat16)
        running = running + grad_codes.astype(jnp.float32) * scale_rows[:, :, None]
        return running, (layer_rows, gate_rows, up_rows)

    pieces = (gate_pre.reshape(N_DP, group_rows, hidden_rows),
              up_pre.reshape(N_DP, group_rows, hidden_rows),
              cotangent.reshape(N_DP, group_rows, full_width))
    start_sum = jnp.zeros((hidden_rows, nblocks, full_width // nblocks), jnp.float32)
    running, (layer_rows, gate_rows, up_rows) = lax.scan(group_step, start_sum, pieces)
    weight_grad = running.reshape(hidden_rows, full_width) * (TOKENS ** -0.5)
    layer_out = layer_rows.reshape(-1, full_width)
    gate_grad = gate_rows.reshape(-1, hidden_rows)
    up_grad = up_rows.reshape(-1, hidden_rows)
    return layer_out, gate_grad, up_grad, weight_grad
```

```python
import jax
import jax.numpy as jnp
from jax import lax
from jax.experimental import pallas as pl
from jax.experimental.pallas import tpu as pltpu
from jax.sharding import PartitionSpec as P

MESH = pl.DeviceIdType.MESH
BF = jnp.bfloat16
F32 = jnp.float32
D = 2560
TOK = 512
UNITS = 1600
WIN = 896
WR = 1008
AR, BR = 576, 432
NSEM = 160
SCALE = float(16384) ** -0.5
ORDER = (4, 3, -3, 2, -2, 1, -1, 0)


def dot(a, b):
    return jnp.dot(a, b, preferred_element_type=F32)


def dot_nt(a, b):
    return lax.dot_general(a, b, (((1,), (1,)), ((), ())), preferred_element_type=F32)


def kernel(
    gate_hbm, up_hbm, codes_ref, scales_ref, cot_in,
    out_ref, gg_ref, ug_ref, wg_ref,
    gate, up, wire, stage, w, cot, hid, hraw, hs, hst, st, g, x_in, ra, rb, fq, fb, res, stage2, stage3,
    lp, lc, ly, lf, lz, lq, dh, dd, dr, ssem, rsem, lsem,
):
    dp, t = lax.axis_index("dp"), lax.axis_index("tensor")
    x, z, y, c = dp // 8, dp % 8, t // 2, t % 2
    half = x // 2
    xb = x % 2
    is_r = c == half
    not_r = c != half
    vb = jnp.where(is_r, xb, 1 - xb)
    zdev = {1: (8 * x + (z + 1) % 8, t), -1: (8 * x + (z + 7) % 8, t)}
    ydev = {1: (dp, 2 * ((y + 1) % 4) + c), -1: (dp, 2 * ((y + 3) % 4) + c)}
    core = (dp, 2 * y + 1 - c)
    qdev = (8 * (x + 1 - 2 * xb) + z, t)
    pdp = 8 * (3 - x) + z
    psame = (pdp, t)
    pother = (pdp, 2 * y + 1 - c)
    pcore = ((pdp, 2 * y), (pdp, 2 * y + 1))

    count = [0]

    def rc(src, dst, dev):
        i = count[0]
        count[0] += 1
        return pltpu.make_async_remote_copy(
            src_ref=src, dst_ref=dst, send_sem=ssem.at[i], recv_sem=rsem.at[i],
            device_id=dev, device_id_type=MESH,
        )

    sent = []

    def start(cp):
        cp.start()
        sent.append(cp)

    load_gate = pltpu.make_async_copy(gate_hbm, gate, lsem.at[0])
    load_up = pltpu.make_async_copy(up_hbm, up, lsem.at[1])
    load_gate.start()
    load_up.start()

    barrier = pltpu.get_barrier_semaphore()
    everyone = (zdev[1], zdev[-1], ydev[1], ydev[-1], core, qdev, psame, pother)
    for dev in everyone:
        pl.semaphore_signal(barrier, inc=1, device_id=dev, device_id_type=MESH)

    left = []
    for p in range(20):
        scale = scales_ref[:, p // 2 : p // 2 + 1]
        piece = codes_ref[:, 128 * p : 128 * p + 128].astype(F32) * scale
        stage[48 * p : 48 * p + 48, :] = piece[:48].astype(BF)
        left.append(piece[48:50])
    left.append(jnp.zeros((8, 128), F32))
    stage[960:1008, :] = jnp.concatenate(left, axis=0).astype(BF)

    pl.semaphore_wait(barrier, len(everyone))

    def blk(b, k):
        return 8 * b + lax.rem(z + k + 8, 8)

    rows_a = pl.ds(0, AR)
    rows_b = pl.ds(AR, BR)
    half_a = {1: pl.ds(0, 288), -1: pl.ds(288, 288)}
    half_b = {1: pl.ds(AR, 224), -1: pl.ds(AR + 224, 208)}
    own_slot = 8 * vb + z

    swap_w = rc(stage, wire.at[8 * xb + z], pother)
    own_w = pltpu.make_async_copy(stage, wire.at[own_slot], lsem.at[2])

    def ring(b, rows, halves):
        return {
            (d, s): rc(
                wire.at[blk(b, -d * (s - 1)), rows if s < 4 else halves[d]],
                wire.at[blk(b, -d * (s - 1)), rows if s < 4 else halves[d]],
                zdev[d],
            )
            for s in (1, 2, 3, 4)
            for d in (1, -1)
        }

    fa = ring(vb, rows_a, half_a)
    fb_own = ring(vb, rows_b, half_b)
    fb_q = ring(1 - vb, rows_b, half_b)
    q_b = rc(wire.at[own_slot, rows_b], wire.at[own_slot, rows_b], qdev)
    q_a = {
        k: rc(wire.at[blk(vb, k), rows_a], wire.at[blk(vb, k), rows_a], qdev)
        for k in (0, 1, -1, 2, -2, 3, -3)
    }
    for d in (1, -1):
        q_a[4, d] = rc(wire.at[blk(vb, 4), half_a[d]], wire.at[blk(vb, 4), half_a[d]], qdev)

    def ag_begin():
        for cp in (q_b, fa[1, 1], fa[-1, 1], fb_own[1, 1], fb_own[-1, 1], q_a[0]):
            cp.start()

    sent.extend((q_b, fa[1, 1], fa[-1, 1], fb_own[1, 1], fb_own[-1, 1], q_a[0]))

    def ag_a(s):
        for d in (1, -1):
            fa[d, s].wait_recv()
            if s < 4:
                start(fa[d, s + 1])
                start(q_a[-d * s])
            else:
                start(q_a[4, d])

    def ag_b(s, which):
        for d in (1, -1):
            which[d, s].wait_recv()
            if s < 4:
                start(which[d, s + 1])

    def crow(gr, tt):
        return pl.multiple_of(512 * gr + 64 * tt, 32)

    def cblk(gr, yy, off=0, n=64):
        return cot.at[pl.ds(pl.multiple_of(512 * gr + 64 * (2 * yy + c) + off, 32), n)]

    y1, ym1, y2 = (y + 1) % 4, (y + 3) % 4, (y + 2) % 4
    cot_p = rc(cot_in, cblk(1, y), psame)
    own_c = pltpu.make_async_copy(cot_in, cblk(0, y), lsem.at[3])
    cot_y, cot_h, cot_core = {}, {}, {}
    for gr in (0, 1):
        mine = cot_in if gr == 0 else cblk(1, y)
        for d in (1, -1):
            cot_y[gr, d] = rc(mine, cblk(gr, y), ydev[d])
        cot_h[gr, 1] = rc(cblk(gr, ym1, 0, 32), cblk(gr, ym1, 0, 32), ydev[1])
        cot_h[gr, -1] = rc(cblk(gr, y1, 32, 32), cblk(gr, y1, 32, 32), ydev[-1])
        cot_core[gr, 0] = rc(mine, cblk(gr, y), core)
        cot_core[gr, 1] = rc(cblk(gr, ym1), cblk(gr, ym1), core)
        cot_core[gr, -1] = rc(cblk(gr, y1), cblk(gr, y1), core)
        cot_core[gr, 2] = rc(cblk(gr, y2, 0, 32), cblk(gr, y2, 0, 32), core)
        cot_core[gr, -2] = rc(cblk(gr, y2, 32, 32), cblk(gr, y2, 32, 32), core)

    def cot_begin(gr):
        for d in (1, -1):
            start(cot_y[gr, d])
        start(cot_core[gr, 0])

    def cot_forward(gr):
        for d in (1, -1):
            cot_y[gr, d].wait_recv()
            start(cot_h[gr, d])
            start(cot_core[gr, d])

    def cot_last(gr):
        for d in (1, -1):
            cot_h[gr, d].wait_recv()
            start(cot_core[gr, 2 * d])

    def cot_end(gr):
        for k in (0, 1, -1, 2, -2):
            cot_core[gr, k].wait_recv()

    def win(h):
        return hid.at[:, 768 * h : 768 * h + WIN]

    hid_p = {h: rc(win(h), hraw.at[1], pcore[h]) for h in (0, 1)}
    hid_core = {h: rc(win(h), hraw.at[0], core) for h in (0, 1)}
    hid_own = {h: pltpu.make_async_copy(win(h), hraw.at[0], lsem.at[4]) for h in (0, 1)}

    def hidden_rows(lo, hi):
        @pl.loop(lo, hi)
        def _(i):
            r = pl.ds(pl.multiple_of(16 * i, 16), 16)
            gv = gate[r, :].astype(F32)
            uv = up[r, :].astype(F32)
            hid[r, 0:UNITS] = (gv * jax.nn.sigmoid(gv) * uv).astype(BF)
            hid[r, UNITS:1664] = jnp.zeros((16, 1664 - UNITS), BF)

    def both(fn):
        for h in (0, 1):
            pl.when(c == h)(lambda h=h: fn(h))

    @pl.when(not_r)
    def _():
        swap_w.start()

    start(cot_p)
    own_c.start()
    cot_begin(0)

    @pl.when(is_r)
    def _():
        own_w.start()
        own_w.wait()
        ag_begin()

    @pl.loop(0, 16)
    def _(b):
        row = lax.broadcasted_iota(jnp.int32, (64, WIN), 0)
        lane = lax.broadcasted_iota(jnp.int32, (64, WIN), 1)
        hit = (lane == row + (32 * c + 50 * b)) & (row < 50)
        st[pl.ds(pl.multiple_of(64 * b, 64), 64), :] = jnp.where(hit, 1.0, 0.0).astype(BF)

    load_gate.wait()
    load_up.wait()
    hidden_rows(0, 8)

    @pl.when(not_r)
    def _():
        swap_w.wait_recv()
        ag_begin()

    hidden_rows(8, 32)

    @pl.when(not_r)
    def _():
        hid_p[0].start()
        hid_p[1].start()

    @pl.when(is_r)
    def _():
        both(lambda h: hid_own[h].start())
        both(lambda h: hid_core[1 - h].start())

    def spread(gr):
        src = hraw.at[gr]
        for b, lo in ((0, 0), (512, 384)):
            sel = st[b : b + 512, lo : lo + 512]
            val = src[:, lo : lo + 512]
            hs[512 * gr : 512 * gr + 512, b : b + 512] = dot_nt(val, sel).astype(BF)
            hst[b : b + 512, 512 * gr : 512 * gr + 512] = dot_nt(sel, val).astype(BF)

    def wgrad():
        @pl.loop(0, 4)
        def _(m):
            left = [[] for _ in range(4)]
            lhs = hst[pl.ds(pl.multiple_of(256 * m, 256), 256), :]
            for n in range(5):
                acc = dot(lhs, cot[:, 512 * n : 512 * n + 512])
                for b in range(4):
                    for j in range(4):
                        p = 4 * n + j
                        col = acc[:, 128 * j : 128 * j + 128]
                        g[4 * m + b, 48 * p : 48 * p + 48, :] = col[64 * b : 64 * b + 48].astype(BF)
                        left[b].append(col[64 * b + 48 : 64 * b + 50])
            for b in range(4):
                tail = jnp.concatenate(left[b] + [jnp.zeros((8, 128), F32)], axis=0)
                g[4 * m + b, 960:1008, :] = tail.astype(BF)

    def unpack():
        @pl.loop(0, 16)
        def _(i):
            base = pl.multiple_of(64 * i, 64)
            tail = wire[i, 960:1008, :].astype(F32)
            for p in range(20):
                cols = slice(128 * p, 128 * p + 128)
                w[pl.ds(base, 48), cols] = wire[i, 48 * p : 48 * p + 48, :]
                last = jnp.concatenate([tail[2 * p : 2 * p + 2], jnp.zeros((14, 128), F32)], axis=0)
                w[pl.ds(base + 48, 16), cols] = last.astype(BF)

    def kidx(k):
        return k + 3

    ga = {k: rc(g.at[blk(1 - vb, k), rows_a], x_in.at[kidx(k)], qdev) for k in ORDER}
    ha = {1: pl.ds(0, 288), -1: pl.ds(288, 288)}
    hb = {1: pl.ds(0, 224), -1: pl.ds(224, 208)}
    ra_c, rb_c = {}, {}
    for s in (1, 2, 3, 4):
        for d in (1, -1):
            if s == 1:
                ra_c[d, s] = rc(x_in.at[kidx(4), ha[d]], ra.at[(1 - d) // 2, 0, ha[d]], zdev[d])
            else:
                ra_c[d, s] = rc(x_in.at[kidx(d * (5 - s))], ra.at[(1 - d) // 2, s - 1], zdev[d])
            for bb, b in ((0, vb), (1, 1 - vb)):
                if s == 1:
                    rb_c[bb, d, s] = rc(g.at[blk(b, 4), half_b[d]], rb.at[bb, (1 - d) // 2, 0, hb[d]], zdev[d])
                else:
                    rb_c[bb, d, s] = rc(g.at[blk(b, d * (5 - s)), rows_b], rb.at[bb, (1 - d) // 2, s - 1], zdev[d])
    fin_q = rc(fq, fb, qdev)
    swap_g = rc(stage2, stage3, pother)

    def add_into(dst, *terms):
        n = dst.shape[0]
        step = 144 if n % 144 == 0 else 16

        @pl.loop(0, n // step)
        def _(i):
            r = pl.ds(pl.multiple_of(i * step, 16), step)
            v = dst[r, :].astype(F32)
            for term in terms:
                v = v + term[r, :].astype(F32)
            dst[r, :] = v.astype(dst.dtype)

    def rs_begin():
        for bb in (1, 0):
            for d in (1, -1):
                start(rb_c[bb, d, 1])
        for k in ORDER:
            start(ga[k])

    def rs_x(k):
        ga[k].wait_recv()
        add_into(x_in.at[kidx(k)], g.at[blk(vb, k), rows_a])

    def rs_a(s):
        if s == 1:
            rs_x(4)
            for d in (1, -1):
                start(ra_c[d, 1])
            return
        for d in (1, -1):
            k = d * (5 - s)
            rs_x(k)
            ra_c[d, s - 1].wait_recv()
            rows = ha[d] if s == 2 else pl.ds(0, AR)
            add_into(x_in.at[kidx(k), rows], ra.at[(1 - d) // 2, s - 2, rows])
            start(ra_c[d, s])

    def rs_b(s):
        for bb, b in ((1, 1 - vb), (0, vb)):
            for d in (1, -1):
                k = d * (5 - s)
                rb_c[bb, d, s - 1].wait_recv()
                if s == 2:
                    dst, src = g.at[blk(b, k), half_b[d]], rb.at[bb, (1 - d) // 2, 0, hb[d]]
                else:
                    dst, src = g.at[blk(b, k), rows_b], rb.at[bb, (1 - d) // 2, s - 2]
                add_into(dst, src)
                start(rb_c[bb, d, s])

    def rs_end():
        for d in (1, -1):
            rb_c[1, d, 4].wait_recv()
        fq[...] = (
            g[blk(1 - vb, 0), rows_b, :].astype(F32)
            + rb[1, 0, 3].astype(F32)
            + rb[1, 1, 3].astype(F32)
        ).astype(BF)
        start(fin_q)
        rs_x(0)
        for d in (1, -1):
            ra_c[d, 4].wait_recv()
            rb_c[0, d, 4].wait_recv()
        res[rows_a, :] = x_in[kidx(0)].astype(F32) + ra[0, 3].astype(F32) + ra[1, 3].astype(F32)
        part = g[blk(vb, 0), rows_b, :].astype(F32) + rb[0, 0, 3].astype(F32) + rb[0, 1, 3].astype(F32)
        fin_q.wait_recv()
        res[rows_b, :] = part + fb[...].astype(F32)

        @pl.when(not_r)
        def _():
            stage2[...] = res[...].astype(BF)
            swap_g.start()
            swap_g.wait_recv()
            res[...] = stage3[...].astype(F32)
            swap_g.wait_send()

        for p in range(20):
            cols = slice(128 * p, 128 * p + 128)
            wg_ref[0:48, cols] = res[48 * p : 48 * p + 48, :] * SCALE
            wg_ref[48:50, cols] = res[960 + 2 * p : 962 + 2 * p, :] * SCALE

    def layer(gr, ch):
        @pl.loop(0, 5)
        def _(n):
            off = pl.multiple_of(256 * n, 256)
            acc = dot(hs[512 * gr : 512 * gr + 512, :], w[:, pl.ds(pl.multiple_of(1280 * ch + off, 256), 256)])
            for tt in range(8):
                r = 64 * (tt // 2)
                lp[gr, ch, tt % 2, r : r + 64, pl.ds(off, 256)] = acc[64 * tt : 64 * tt + 64].astype(BF)

    l_core, l_y1, l_y2, l_p = {}, {}, {}, {}

    def yrow(yy, off=0, n=64):
        return pl.ds(pl.multiple_of(64 * yy + off, 32), n)

    for gr in (1, 0):
        for ch in (0, 1):
            l_core[gr, ch] = rc(lp.at[gr, ch, 1 - c], lc.at[gr, ch], core)
            for d in (1, -1):
                o = 0 if d == 1 else 32
                l_y1[gr, ch, d] = rc(lc.at[gr, ch, yrow(y2, o, 32)], ly.at[gr, ch, (1 - d) // 2], ydev[d])
                to = y1 if d == 1 else ym1
                l_y2[gr, ch, d] = rc(lc.at[gr, ch, yrow(to)], lf.at[gr, ch, (1 - d) // 2], ydev[d])
    for ch in (0, 1):
        l_p[ch] = rc(lz.at[ch], lq.at[ch], psame)

    def layer_core(gr, ch):
        l_core[gr, ch].wait_recv()
        add_into(lc.at[gr, ch], lp.at[gr, ch, c])
        for d in (1, -1):
            start(l_y1[gr, ch, d])

    def layer_y(gr, ch):
        for d in (1, -1):
            l_y1[gr, ch, d].wait_recv()
            o = 0 if d == 1 else 32
            to = y1 if d == 1 else ym1
            add_into(lc.at[gr, ch, yrow(to, o, 32)], ly.at[gr, ch, (1 - d) // 2])
            start(l_y2[gr, ch, d])

    def layer_end(gr, ch):
        for d in (1, -1):
            l_y2[gr, ch, d].wait_recv()
        total = lc[gr, ch, yrow(y), :].astype(F32) + lf[gr, ch, 0].astype(F32) + lf[gr, ch, 1].astype(F32)
        if gr == 1:
            lz[ch] = total.astype(BF)
            start(l_p[ch])
        else:
            l_p[ch].wait_recv()
            out_ref[:, 1280 * ch : 1280 * ch + 1280] = (total + lq[ch].astype(F32)).astype(BF)

    d_p = {}
    d_p["same"] = {h: rc(dd.at[1], dr.at[h], psame) for h in (0, 1)}
    d_p["other"] = {h: rc(dd.at[1], dr.at[h], pother) for h in (0, 1)}
    d_core = {h: rc(dd.at[0], dr.at[h], core) for h in (0, 1)}
    d_own = {h: pltpu.make_async_copy(dd.at[0], dr.at[h], lsem.at[5]) for h in (0, 1)}

    def dhidden(gr):
        @pl.loop(0, 4)
        def _(n):
            off = pl.multiple_of(256 * n, 256)
            dh[:, pl.ds(off, 256)] = dot_nt(cot[512 * gr : 512 * gr + 512, :], w[pl.ds(off, 256), :]).astype(BF)

        a = dot(dh[:, 0:512], st[0:512, 0:512])
        b = dot(dh[:, 512:1024], st[512:1024, 384:896])
        dd[gr, :, 0:384] = a[:, 0:384].astype(BF)
        dd[gr, :, 384:512] = (a[:, 384:512] + b[:, 0:128]).astype(BF)
        dd[gr, :, 512:896] = b[:, 128:512].astype(BF)

    def d_send_p():
        @pl.when(is_r)
        def _():
            both(lambda h: d_p["same"][h].start())

        @pl.when(not_r)
        def _():
            both(lambda h: d_p["other"][h].start())

    def d_send_core():
        @pl.when(is_r)
        def _():
            both(lambda h: d_own[h].start())

        @pl.when(not_r)
        def _():
            both(lambda h: d_core[h].start())

    def d_recv():
        @pl.when(is_r)
        def _():
            both(lambda h: d_own[h].wait())
            both(lambda h: d_core[1 - h].wait_recv())

        @pl.when(not_r)
        def _():
            def arrive(h):
                d_p["same"][h].wait_recv()
                d_p["other"][1 - h].wait_recv()

            both(arrive)

    def d_sent():
        @pl.when(is_r)
        def _():
            both(lambda h: d_p["same"][h].wait_send())

        @pl.when(not_r)
        def _():
            both(lambda h: d_p["other"][h].wait_send())
            both(lambda h: d_core[h].wait_send())

    def grads():
        @pl.loop(0, 32)
        def _(i):
            r = pl.ds(pl.multiple_of(16 * i, 16), 16)

            def write(dv, lo, hi):
                gv = gate[r, lo:hi].astype(F32)
                uv = up[r, lo:hi].astype(F32)
                sv = jax.nn.sigmoid(gv)
                gg_ref[r, lo:hi] = (dv * uv * sv * (1.0 + gv * (1.0 - sv))).astype(BF)
                ug_ref[r, lo:hi] = (dv * (gv * sv)).astype(BF)

            write(dr[0, r, 0:768].astype(F32), 0, 768)
            write(dr[0, r, 768:896].astype(F32) + dr[1, r, 0:128].astype(F32), 768, 896)
            write(dr[1, r, 128:832].astype(F32), 896, 1600)

    ag_a(1)
    cot_forward(0)
    ag_b(1, fb_own)
    q_b.wait_recv()
    for d in (1, -1):
        start(fb_q[d, 1])

    cot_p.wait_recv()
    cot_begin(1)
    ag_a(2)
    cot_last(0)

    @pl.when(is_r)
    def _():
        both(lambda h: hid_own[h].wait())

    @pl.when(not_r)
    def _():
        both(lambda h: hid_core[h].wait_recv())

    spread(0)
    ag_b(2, fb_own)
    ag_b(1, fb_q)
    cot_forward(1)
    ag_a(3)
    ag_b(3, fb_own)
    ag_b(2, fb_q)
    cot_last(1)
    cot_end(0)
    cot_end(1)
    own_c.wait()
    ag_a(4)
    ag_b(4, fb_own)
    ag_b(3, fb_q)

    both(lambda h: hid_p[h].wait_recv())
    spread(1)
    ag_b(4, fb_q)
    wgrad()
    rs_begin()
    for k in (0, 1, -1, 2, -2, 3, -3):
        q_a[k].wait_recv()
    for d in (1, -1):
        q_a[4, d].wait_recv()
    unpack()
    rs_a(1)
    dhidden(1)
    d_send_p()
    rs_b(2)
    layer(1, 0)
    start(l_core[1, 0])
    rs_a(2)
    layer(1, 1)
    start(l_core[1, 1])
    layer_core(1, 0)
    rs_b(3)
    layer_core(1, 1)
    rs_a(3)
    layer_y(1, 0)
    dhidden(0)
    d_send_core()
    layer_y(1, 1)
    rs_b(4)
    layer(0, 0)
    start(l_core[0, 0])
    layer(0, 1)
    start(l_core[0, 1])
    layer_end(1, 0)
    layer_end(1, 1)
    layer_core(0, 0)
    layer_core(0, 1)
    rs_a(4)
    layer_y(0, 0)
    layer_y(0, 1)
    d_recv()
    grads()
    rs_end()
    layer_end(0, 0)
    layer_end(0, 1)

    for cp in sent:
        cp.wait_send()

    @pl.when(not_r)
    def _():
        swap_w.wait_send()
        hid_p[0].wait_send()
        hid_p[1].wait_send()

    @pl.when(is_r)
    def _():
        both(lambda h: hid_core[1 - h].wait_send())

    d_sent()


def body(gate_pre, up_pre, down_codes, down_scales, cotangent):
    vmem = pl.BlockSpec(memory_space=pltpu.VMEM)
    anywhere = pl.BlockSpec(memory_space=pl.ANY)
    return pl.pallas_call(
        kernel,
        out_shape=(
            jax.ShapeDtypeStruct((64, D), BF),
            jax.ShapeDtypeStruct((TOK, UNITS), BF),
            jax.ShapeDtypeStruct((TOK, UNITS), BF),
            jax.ShapeDtypeStruct((50, D), F32),
        ),
        in_specs=[anywhere, anywhere, vmem, vmem, vmem],
        out_specs=(vmem, vmem, vmem, vmem),
        scratch_shapes=[
            pltpu.VMEM((TOK, UNITS), BF),
            pltpu.VMEM((TOK, UNITS), BF),
            pltpu.VMEM((16, WR, 128), BF),
            pltpu.VMEM((WR, 128), BF),
            pltpu.VMEM((1024, D), BF),
            pltpu.VMEM((1024, D), BF),
            pltpu.VMEM((TOK, 1664), BF),
            pltpu.VMEM((2, TOK, WIN), BF),
            pltpu.VMEM((1024, 1024), BF),
            pltpu.VMEM((1024, 1024), BF),
            pltpu.VMEM((1024, WIN), BF),
            pltpu.VMEM((16, WR, 128), BF),
            pltpu.VMEM((8, AR, 128), BF),
            pltpu.VMEM((2, 4, AR, 128), BF),
            pltpu.VMEM((2, 2, 4, BR, 128), BF),
            pltpu.VMEM((BR, 128), BF),
            pltpu.VMEM((BR, 128), BF),
            pltpu.VMEM((WR, 128), F32),
            pltpu.VMEM((WR, 128), BF),
            pltpu.VMEM((WR, 128), BF),
            pltpu.VMEM((2, 2, 2, 256, 1280), BF),
            pltpu.VMEM((2, 2, 256, 1280), BF),
            pltpu.VMEM((2, 2, 2, 32, 1280), BF),
            pltpu.VMEM((2, 2, 2, 64, 1280), BF),
            pltpu.VMEM((2, 64, 1280), BF),
            pltpu.VMEM((2, 64, 1280), BF),
            pltpu.VMEM((TOK, 1024), BF),
            pltpu.VMEM((2, TOK, WIN), BF),
            pltpu.VMEM((2, TOK, WIN), BF),
            pltpu.SemaphoreType.DMA((NSEM,)),
            pltpu.SemaphoreType.DMA((NSEM,)),
            pltpu.SemaphoreType.DMA((8,)),
        ],
        compiler_params=pltpu.CompilerParams(
            collective_id=0, has_side_effects=True, vmem_limit_bytes=62 << 20
        ),
        cost_estimate=pl.CostEstimate(flops=25_000_000_000, bytes_accessed=10_000_000, transcendentals=2_000_000),
    )(gate_pre, up_pre, down_codes, down_scales, cotangent)


def solution(mesh):
    return jax.shard_map(
        body,
        mesh=mesh,
        in_specs=(
            P("dp", "tensor"),
            P("dp", "tensor"),
            P(("tensor", "dp"), None),
            P(("tensor", "dp"), None),
            P(("dp", "tensor"), None),
        ),
        out_specs=(
            P(("dp", "tensor"), None),
            P("dp", "tensor"),
            P("dp", "tensor"),
            P(("tensor", "dp"), None),
        ),
        check_vma=False,
    )
```

```python
import jax
import jax.numpy as jnp
from jax import lax
from jax.experimental import pallas as pl
from jax.experimental.pallas import tpu as pltpu
from jax.sharding import PartitionSpec as P

MESH = pl.DeviceIdType.MESH
BF = jnp.bfloat16
F32 = jnp.float32
D = 2560
TOK = 512
UNITS = 1600
HALF = 800
WR = 1008
AR, BR = 576, 432
AG, BG = 480, 528
NSEM = 160
SCALE = float(16384) ** -0.5
ORDER = (4, 3, -3, 2, -2, 1, -1, 0)


def dot(a, b):
    return jnp.dot(a, b, preferred_element_type=F32)


def dot_nt(a, b):
    return lax.dot_general(a, b, (((1,), (1,)), ((), ())), preferred_element_type=F32)


def kernel(
    gate_hbm, up_hbm, codes_ref, scales_ref, cot_in,
    out_ref, dr, res,
    gate, up, wire, stage, w, cot, hid, ht, hs, eye, g, x_in, ra, rb, fq, fb, stage2, stage3,
    lp, lc, ly, lf, lz, lq, dd, ssem, rsem, lsem,
):
    dp, t = lax.axis_index("dp"), lax.axis_index("tensor")
    x, z, y, c = dp // 8, dp % 8, t // 2, t % 2
    half = x // 2
    xb = x % 2
    is_r = c == half
    not_r = c != half
    vb = jnp.where(is_r, xb, 1 - xb)
    zdev = {1: (8 * x + (z + 1) % 8, t), -1: (8 * x + (z + 7) % 8, t)}
    ydev = {1: (dp, 2 * ((y + 1) % 4) + c), -1: (dp, 2 * ((y + 3) % 4) + c)}
    core = (dp, 2 * y + 1 - c)
    qdev = (8 * (x + 1 - 2 * xb) + z, t)
    pdp = 8 * (3 - x) + z
    psame = (pdp, t)
    pother = (pdp, 2 * y + 1 - c)
    pcore = ((pdp, 2 * y), (pdp, 2 * y + 1))

    count = [0]

    def rc(src, dst, dev):
        i = count[0]
        count[0] += 1
        return pltpu.make_async_remote_copy(
            src_ref=src, dst_ref=dst, send_sem=ssem.at[i], recv_sem=rsem.at[i],
            device_id=dev, device_id_type=MESH,
        )

    sent = []

    def start(cp):
        cp.start()
        sent.append(cp)

    load_gate = pltpu.make_async_copy(gate_hbm, gate, lsem.at[0])
    load_up = pltpu.make_async_copy(up_hbm, up, lsem.at[1])
    load_gate.start()
    load_up.start()

    barrier = pltpu.get_barrier_semaphore()
    everyone = (zdev[1], zdev[-1], ydev[1], ydev[-1], core, qdev, psame, pother)
    for dev in everyone:
        pl.semaphore_signal(barrier, inc=1, device_id=dev, device_id_type=MESH)

    left = []
    for p in range(20):
        scale = scales_ref[:, p // 2 : p // 2 + 1]
        piece = codes_ref[:, 128 * p : 128 * p + 128].astype(F32) * scale
        stage[48 * p : 48 * p + 48, :] = piece[:48].astype(BF)
        left.append(piece[48:50])
    left.append(jnp.zeros((8, 128), F32))
    stage[960:1008, :] = jnp.concatenate(left, axis=0).astype(BF)

    pl.semaphore_wait(barrier, len(everyone))

    def blk(b, k):
        return 8 * b + lax.rem(z + k + 8, 8)

    rows_a = slice(0, AR)
    rows_b = slice(AR, WR)
    half_a = {1: pl.ds(0, 288), -1: pl.ds(288, 288)}
    half_b = {1: pl.ds(AR, 224), -1: pl.ds(AR + 224, 208)}
    own_slot = 8 * vb + z

    swap_w = rc(stage, wire.at[8 * xb + z], pother)
    own_w = pltpu.make_async_copy(stage, wire.at[own_slot], lsem.at[2])

    def ring(b, rows, halves):
        return {
            (d, s): rc(
                wire.at[blk(b, -d * (s - 1)), rows if s < 4 else halves[d]],
                wire.at[blk(b, -d * (s - 1)), rows if s < 4 else halves[d]],
                zdev[d],
            )
            for s in (1, 2, 3, 4)
            for d in (1, -1)
        }

    fa = ring(vb, rows_a, half_a)
    fb_own = ring(vb, rows_b, half_b)
    fb_q = ring(1 - vb, rows_b, half_b)
    q_b = rc(wire.at[own_slot, rows_b], wire.at[own_slot, rows_b], qdev)
    q_a = {
        k: rc(wire.at[blk(vb, k), rows_a], wire.at[blk(vb, k), rows_a], qdev)
        for k in (0, 1, -1, 2, -2, 3, -3)
    }
    for d in (1, -1):
        q_a[4, d] = rc(wire.at[blk(vb, 4), half_a[d]], wire.at[blk(vb, 4), half_a[d]], qdev)

    def ag_begin():
        for cp in (q_b, fa[1, 1], fa[-1, 1], fb_own[1, 1], fb_own[-1, 1], q_a[0]):
            cp.start()

    sent.extend((q_b, fa[1, 1], fa[-1, 1], fb_own[1, 1], fb_own[-1, 1], q_a[0]))

    def ag_a(s):
        for d in (1, -1):
            fa[d, s].wait_recv()
            if s < 4:
                start(fa[d, s + 1])
                start(q_a[-d * s])
            else:
                start(q_a[4, d])

    def ag_b(s, which):
        for d in (1, -1):
            which[d, s].wait_recv()
            if s < 4:
                start(which[d, s + 1])

    def crow(gr, tt):
        return pl.multiple_of(512 * gr + 64 * tt, 32)

    def cblk(gr, yy, off=0, n=64):
        return cot.at[pl.ds(pl.multiple_of(512 * gr + 64 * (2 * yy + c) + off, 32), n)]

    y1, ym1, y2 = (y + 1) % 4, (y + 3) % 4, (y + 2) % 4
    cot_p = {
        o: rc(cot_in.at[pl.ds(o, 32)], cblk(1, y, o, 32), psame) for o in (0, 32)
    }
    own_c = pltpu.make_async_copy(cot_in, cblk(0, y), lsem.at[3])
    cot_y, cot_h, cot_core = {}, {}, {}
    first = {1: 0, -1: 32}
    for gr in (0, 1):
        for d in (1, -1):
            for o in (0, 32):
                mine = cot_in.at[pl.ds(o, 32)] if gr == 0 else cblk(1, y, o, 32)
                cot_y[gr, d, o] = rc(mine, cblk(gr, y, o, 32), ydev[d])
        cot_h[gr, 1] = rc(cblk(gr, ym1, 0, 32), cblk(gr, ym1, 0, 32), ydev[1])
        cot_h[gr, -1] = rc(cblk(gr, y1, 32, 32), cblk(gr, y1, 32, 32), ydev[-1])
        mine = cot_in if gr == 0 else cblk(1, y)
        cot_core[gr, 0] = rc(mine, cblk(gr, y), core)
        cot_core[gr, 1] = rc(cblk(gr, ym1), cblk(gr, ym1), core)
        cot_core[gr, -1] = rc(cblk(gr, y1), cblk(gr, y1), core)
        cot_core[gr, 2] = rc(cblk(gr, y2, 0, 32), cblk(gr, y2, 0, 32), core)
        cot_core[gr, -2] = rc(cblk(gr, y2, 32, 32), cblk(gr, y2, 32, 32), core)

    def cot_begin():
        for o in (0, 1):
            for d in (1, -1):
                start(cot_y[0, d, first[d] if o == 0 else 32 - first[d]])
        start(cot_core[0, 0])

    def cot_partner():
        for o in (0, 32):
            cot_p[o].wait_recv()
        for o in (0, 1):
            for d in (1, -1):
                start(cot_y[1, d, first[d] if o == 0 else 32 - first[d]])
        start(cot_core[1, 0])

    def cot_forward(gr):
        for d in (1, -1):
            cot_y[gr, d, first[d]].wait_recv()
            start(cot_h[gr, d])

    def cot_rest(gr):
        for d in (1, -1):
            cot_y[gr, d, 32 - first[d]].wait_recv()
            start(cot_core[gr, d])

    def cot_last(gr):
        for d in (1, -1):
            cot_h[gr, d].wait_recv()
            start(cot_core[gr, 2 * d])

    def cot_end(gr):
        for k in (0, 1, -1, 2, -2):
            cot_core[gr, k].wait_recv()

    def rows_of(h, b):
        return pl.ds(pl.multiple_of(HALF * h + 400 * b, 16), 400)

    def cols_of(gr):
        return slice(512 * gr, 512 * gr + 512)

    hid_p, hid_core, hid_own = {}, {}, {}
    for h in (0, 1):
        v_to = jnp.where(h == 1 - half, 1 - xb, xb)
        for o in (0, 1):
            b = 1 - v_to if o == 0 else v_to
            hid_p[h, o] = rc(hid.at[rows_of(h, b)], ht.at[rows_of(0, b), cols_of(1)], pcore[h])
    for h in (0, 1):
        whole = hid.at[HALF * h : HALF * h + HALF]
        hid_core[h] = rc(whole, ht.at[:, cols_of(0)], core)
        hid_own[h] = pltpu.make_async_copy(whole, ht.at[:, cols_of(0)], lsem.at[4])

    def hidden_rows(lo, hi):
        @pl.loop(lo, hi)
        def _(i):
            r = pl.ds(pl.multiple_of(32 * i, 32), 32)
            gv = gate[r, :].astype(F32)
            uv = up[r, :].astype(F32)
            hid[r, :] = (gv * jax.nn.sigmoid(gv) * uv).astype(BF)

    def both(fn):
        for h in (0, 1):
            pl.when(c == h)(lambda h=h: fn(h))

    def cot_to_partner():
        for o in (0, 32):
            cot_p[o].start()

    sent.extend(cot_p.values())

    @pl.when(not_r)
    def _():
        swap_w.start()
        cot_to_partner()

    own_c.start()
    cot_begin()

    @pl.when(is_r)
    def _():
        own_w.start()
        own_w.wait()
        ag_begin()

    row = lax.broadcasted_iota(jnp.int32, (TOK, TOK), 0)
    lane = lax.broadcasted_iota(jnp.int32, (TOK, TOK), 1)
    eye[...] = jnp.where(row == lane, 1.0, 0.0).astype(BF)

    load_gate.wait()
    load_up.wait()
    hidden_rows(0, 15)

    pl.when(is_r)(cot_to_partner)

    @pl.when(not_r)
    def _():
        swap_w.wait_recv()
        ag_begin()

    hidden_rows(15, 50)

    @pl.when(not_r)
    def _():
        for o in (0, 1):
            for h in (0, 1):
                hid_p[h, o].start()

    @pl.when(is_r)
    def _():
        both(lambda h: hid_own[h].start())
        both(lambda h: hid_core[1 - h].start())

    def turn(gr):
        hs[512 * gr : 512 * gr + 512, :] = dot_nt(eye[...], ht[:, cols_of(gr)]).astype(BF)

    def wgrad(b):
        left = [[] for _ in range(8)]
        lhs = ht[pl.ds(pl.multiple_of(400 * b, 16), 400), :]
        for n in range(5):
            acc = dot(lhs, cot[:, 512 * n : 512 * n + 512])
            for i in range(8):
                for j in range(4):
                    p = 4 * n + j
                    col = acc[50 * i : 50 * i + 50, 128 * j : 128 * j + 128]
                    g[8 * b + i, 48 * p : 48 * p + 48, :] = col[:48].astype(BF)
                    left[i].append(col[48:50])
        for i in range(8):
            tail = jnp.concatenate(left[i] + [jnp.zeros((8, 128), F32)], axis=0)
            g[8 * b + i, 960:1008, :] = tail.astype(BF)

    def unpack(b):
        tails = [wire[8 * b + i, 960:1008, :].astype(F32) for i in range(8)]
        for p in range(20):
            rows = []
            for i in range(8):
                rows.append(wire[8 * b + i, 48 * p : 48 * p + 48, :].astype(F32))
                rows.append(tails[i][2 * p : 2 * p + 2])
            w[pl.ds(pl.multiple_of(400 * b, 16), 400), 128 * p : 128 * p + 128] = jnp.concatenate(rows, axis=0).astype(BF)

    cut_a, cut_b = slice(0, AG), slice(AG, WR)
    part_b = {1: pl.ds(AG, 272), -1: pl.ds(AG + 272, 256)}

    def kidx(k):
        return k + 3

    ga = {k: rc(g.at[blk(1 - vb, k), cut_a], x_in.at[kidx(k)], qdev) for k in ORDER}
    ha = {1: pl.ds(0, 240), -1: pl.ds(240, 240)}
    hb = {1: pl.ds(0, 272), -1: pl.ds(272, 256)}
    ra_c, rb_c = {}, {}
    for s in (1, 2, 3, 4):
        for d in (1, -1):
            if s == 1:
                ra_c[d, s] = rc(x_in.at[kidx(4), ha[d]], ra.at[(1 - d) // 2, 0, ha[d]], zdev[d])
            else:
                ra_c[d, s] = rc(x_in.at[kidx(d * (5 - s))], ra.at[(1 - d) // 2, s - 1], zdev[d])
            for bb, b in ((0, vb), (1, 1 - vb)):
                if s == 1:
                    rb_c[bb, d, s] = rc(g.at[blk(b, 4), part_b[d]], rb.at[bb, (1 - d) // 2, 0, hb[d]], zdev[d])
                else:
                    rb_c[bb, d, s] = rc(g.at[blk(b, d * (5 - s)), cut_b], rb.at[bb, (1 - d) // 2, s - 1], zdev[d])
    fin_q = rc(fq, fb, qdev)
    swap_ga = rc(stage2.at[cut_a], stage3.at[cut_a], pother)
    swap_gb = rc(stage2.at[cut_b], stage3.at[cut_b], pother)

    def add_into(dst, *terms):
        n = dst.shape[0]
        step = next(v for v in (176, 160, 136, 128, 120, 32, 16) if n % v == 0 and v % 16 == 0)

        @pl.loop(0, n // step)
        def _(i):
            r = pl.ds(pl.multiple_of(i * step, 16), step)
            v = dst[r, :].astype(F32)
            for term in terms:
                v = v + term[r, :].astype(F32)
            dst[r, :] = v.astype(dst.dtype)

    def rs_begin(bb):
        for d in (1, -1):
            start(rb_c[bb, d, 1])
        if bb == 1:
            start(ga[4])

    def rs_x(k):
        ga[k].wait_recv()
        add_into(x_in.at[kidx(k)], g.at[blk(vb, k), cut_a])

    def rs_first():
        rs_x(4)
        for d in (1, -1):
            start(ra_c[d, 1])

    def rs_a(s, d):
        k = d * (5 - s)
        rs_x(k)
        ra_c[d, s - 1].wait_recv()
        rows = ha[d] if s == 2 else pl.ds(0, AG)
        add_into(x_in.at[kidx(k), rows], ra.at[(1 - d) // 2, s - 2, rows])
        start(ra_c[d, s])

    def rs_b(bb, s):
        b = 1 - vb if bb == 1 else vb
        for d in (1, -1):
            k = d * (5 - s)
            rb_c[bb, d, s - 1].wait_recv()
            if s == 2:
                dst, src = g.at[blk(b, k), part_b[d]], rb.at[bb, (1 - d) // 2, 0, hb[d]]
            else:
                dst, src = g.at[blk(b, k), cut_b], rb.at[bb, (1 - d) // 2, s - 2]
            add_into(dst, src)
            start(rb_c[bb, d, s])

    def rs_b_other():
        for d in (1, -1):
            rb_c[1, d, 4].wait_recv()
        fq[...] = (
            g[blk(1 - vb, 0), cut_b, :].astype(F32)
            + rb[1, 0, 3].astype(F32)
            + rb[1, 1, 3].astype(F32)
        ).astype(BF)
        start(fin_q)

    def swap_out(rows, cp, total):
        res[rows, :] = total

        @pl.when(not_r)
        def _():
            stage2[rows, :] = total.astype(BF)
            cp.start()

    def rs_b_end():
        for d in (1, -1):
            rb_c[0, d, 4].wait_recv()
        part = g[blk(vb, 0), cut_b, :].astype(F32) + rb[0, 0, 3].astype(F32) + rb[0, 1, 3].astype(F32)
        fin_q.wait_recv()
        swap_out(cut_b, swap_gb, part + fb[...].astype(F32))

    def rs_a_end():
        for d in (1, -1):
            ra_c[d, 4].wait_recv()
        total = x_in[kidx(0)].astype(F32) + ra[0, 3].astype(F32) + ra[1, 3].astype(F32)
        swap_out(cut_a, swap_ga, total)

    def rs_end():
        @pl.when(not_r)
        def _():
            swap_gb.wait_recv()
            res[cut_b, :] = stage3[cut_b, :].astype(F32)
            swap_ga.wait_recv()
            res[cut_a, :] = stage3[cut_a, :].astype(F32)
            swap_ga.wait_send()
            swap_gb.wait_send()

    def layer(gr, ch):
        @pl.loop(0, 5)
        def _(n):
            off = pl.multiple_of(256 * n, 256)
            acc = dot(hs[512 * gr : 512 * gr + 512, :], w[:, pl.ds(pl.multiple_of(1280 * ch + off, 256), 256)])
            for tt in range(8):
                r = 64 * (tt // 2)
                lp[gr, ch, tt % 2, r : r + 64, pl.ds(off, 256)] = acc[64 * tt : 64 * tt + 64].astype(BF)

    l_core, l_y1, l_y2, l_p = {}, {}, {}, {}

    def yrow(yy, off=0, n=64):
        return pl.ds(pl.multiple_of(64 * yy + off, 32), n)

    for gr in (1, 0):
        for ch in (0, 1):
            l_core[gr, ch] = rc(lp.at[gr, ch, 1 - c], lc.at[gr, ch], core)
            for d in (1, -1):
                o = 0 if d == 1 else 32
                l_y1[gr, ch, d] = rc(lc.at[gr, ch, yrow(y2, o, 32)], ly.at[gr, ch, (1 - d) // 2], ydev[d])
                to = y1 if d == 1 else ym1
                l_y2[gr, ch, d] = rc(lc.at[gr, ch, yrow(to)], lf.at[gr, ch, (1 - d) // 2], ydev[d])
    for ch in (0, 1):
        l_p[ch] = rc(lz.at[ch], lq.at[ch], psame)

    def layer_core(gr, ch):
        l_core[gr, ch].wait_recv()
        add_into(lc.at[gr, ch], lp.at[gr, ch, c])
        for d in (1, -1):
            start(l_y1[gr, ch, d])

    def layer_y(gr, ch):
        for d in (1, -1):
            l_y1[gr, ch, d].wait_recv()
            o = 0 if d == 1 else 32
            to = y1 if d == 1 else ym1
            add_into(lc.at[gr, ch, yrow(to, o, 32)], ly.at[gr, ch, (1 - d) // 2])
            start(l_y2[gr, ch, d])

    def layer_end(gr, ch):
        for d in (1, -1):
            l_y2[gr, ch, d].wait_recv()
        total = lc[gr, ch, yrow(y), :].astype(F32) + lf[gr, ch, 0].astype(F32) + lf[gr, ch, 1].astype(F32)
        if gr == 1:
            lz[ch] = total.astype(BF)
            start(l_p[ch])
        else:
            l_p[ch].wait_recv()
            out_ref[:, 1280 * ch : 1280 * ch + 1280] = (total + lq[ch].astype(F32)).astype(BF)

    def drows(h, q):
        return pl.ds(HALF * h + 400 * q, 400)

    d_p, d_core, d_own = {}, {}, {}
    for h in (0, 1):
        for q in (0, 1):
            src = dd.at[1, 400 * q : 400 * q + 400]
            d_p["same", h, q] = rc(src, dr.at[drows(h, q)], psame)
            d_p["other", h, q] = rc(src, dr.at[drows(h, q)], pother)
            src = dd.at[0, 400 * q : 400 * q + 400]
            d_core[h, q] = rc(src, dr.at[drows(h, q)], core)
            d_own[h, q] = pltpu.make_async_copy(src, dr.at[drows(h, q)], lsem.at[5 + q])

    def dhidden(gr, q):
        dd[gr, 400 * q : 400 * q + 400, :] = dot_nt(
            w[400 * q : 400 * q + 400, :], cot[512 * gr : 512 * gr + 512, :]
        ).astype(BF)

    def d_send_p(q):
        @pl.when(is_r)
        def _():
            both(lambda h: d_p["same", h, q].start())

        @pl.when(not_r)
        def _():
            both(lambda h: d_p["other", h, q].start())

    def d_send_core(q):
        @pl.when(is_r)
        def _():
            both(lambda h: d_own[h, q].start())

        @pl.when(not_r)
        def _():
            both(lambda h: d_core[h, q].start())

    def d_recv(q):
        @pl.when(is_r)
        def _():
            both(lambda h: d_own[h, q].wait())
            both(lambda h: d_core[1 - h, q].wait_recv())

        @pl.when(not_r)
        def _():
            def arrive(h):
                d_p["same", h, q].wait_recv()
                d_p["other", 1 - h, q].wait_recv()

            both(arrive)

    def d_sent():
        for q in (0, 1):
            @pl.when(is_r)
            def _():
                both(lambda h: d_p["same", h, q].wait_send())

            @pl.when(not_r)
            def _():
                both(lambda h: d_p["other", h, q].wait_send())
                both(lambda h: d_core[h, q].wait_send())

    q_b.wait_recv()
    for d in (1, -1):
        start(fb_q[d, 1])
    ag_a(1)
    cot_forward(0)

    @pl.when(is_r)
    def _():
        both(lambda h: hid_own[h].wait())

    @pl.when(not_r)
    def _():
        both(lambda h: hid_core[h].wait_recv())

    turn(0)
    ag_b(1, fb_own)
    cot_partner()
    ag_b(1, fb_q)
    cot_rest(0)
    cot_last(0)
    ag_a(2)
    cot_forward(1)
    ag_b(2, fb_own)
    ag_b(2, fb_q)
    cot_rest(1)
    ag_a(3)
    cot_last(1)
    ag_b(3, fb_own)
    cot_end(0)
    cot_end(1)
    own_c.wait()
    both(lambda h: hid_p[h, 0].wait_recv())
    wgrad(1 - vb)
    rs_begin(1)
    ag_b(3, fb_q)
    ag_a(4)
    for k in ORDER[1:]:
        start(ga[k])
    both(lambda h: hid_p[h, 1].wait_recv())
    wgrad(vb)
    rs_begin(0)
    ag_b(4, fb_own)
    ag_b(4, fb_q)
    rs_b(1, 2)
    turn(1)
    rs_first()
    for k in (0, 1, -1, 2, -2, 3, -3):
        q_a[k].wait_recv()
    for d in (1, -1):
        q_a[4, d].wait_recv()
    unpack(0)
    unpack(1)
    layer(1, 0)
    start(l_core[1, 0])
    rs_b(0, 2)
    dhidden(1, 0)
    d_send_p(0)
    layer_core(1, 0)
    rs_a(2, 1)
    dhidden(1, 1)
    d_send_p(1)
    rs_b(1, 3)
    rs_a(2, -1)
    layer(1, 1)
    start(l_core[1, 1])
    rs_b(0, 3)
    layer_y(1, 0)
    dhidden(0, 0)
    d_send_core(0)
    rs_a(3, 1)
    layer_core(1, 1)
    rs_b(1, 4)
    rs_a(3, -1)
    dhidden(0, 1)
    d_send_core(1)
    layer(0, 0)
    start(l_core[0, 0])
    rs_b(0, 4)
    layer_y(1, 1)
    rs_a(4, 1)
    layer(0, 1)
    start(l_core[0, 1])
    layer_core(0, 0)
    rs_a(4, -1)
    layer_end(1, 0)
    rs_b_other()
    layer_core(0, 1)
    layer_y(0, 0)
    layer_end(1, 1)
    rs_x(0)
    layer_y(0, 1)
    rs_b_end()
    rs_a_end()
    d_recv(0)
    d_recv(1)
    layer_end(0, 0)
    layer_end(0, 1)
    rs_end()

    for cp in sent:
        cp.wait_send()

    @pl.when(not_r)
    def _():
        swap_w.wait_send()
        for o in (0, 1):
            for h in (0, 1):
                hid_p[h, o].wait_send()

    @pl.when(is_r)
    def _():
        both(lambda h: hid_core[1 - h].wait_send())

    d_sent()


def last_kernel(dr, gate, up, out_in, res, gg_ref, ug_ref, out_ref, wg_ref):
    dv = dr[...].astype(F32)
    gv = gate[...].astype(F32)
    uv = up[...].astype(F32)
    sv = jax.nn.sigmoid(gv)
    gg_ref[...] = (dv * uv * sv * (1.0 + gv * (1.0 - sv))).astype(BF)
    ug_ref[...] = (dv * (gv * sv)).astype(BF)

    @pl.when(pl.program_id(0) == 0)
    def _():
        out_ref[...] = out_in[...]
        for p in range(20):
            cols = slice(128 * p, 128 * p + 128)
            wg_ref[0:48, cols] = res[48 * p : 48 * p + 48, :] * SCALE
            wg_ref[48:50, cols] = res[960 + 2 * p : 962 + 2 * p, :] * SCALE


def body(gate_pre, up_pre, down_codes, down_scales, cotangent):
    vmem = pl.BlockSpec(memory_space=pltpu.VMEM)
    anywhere = pl.BlockSpec(memory_space=pl.ANY)
    gate_t, up_t = gate_pre.T, up_pre.T
    out, dhid, total = pl.pallas_call(
        kernel,
        out_shape=(
            jax.ShapeDtypeStruct((64, D), BF),
            jax.ShapeDtypeStruct((UNITS, TOK), BF),
            jax.ShapeDtypeStruct((WR, 128), F32),
        ),
        in_specs=[anywhere, anywhere, vmem, vmem, vmem],
        out_specs=(vmem, vmem, vmem),
        scratch_shapes=[
            pltpu.VMEM((UNITS, TOK), BF),
            pltpu.VMEM((UNITS, TOK), BF),
            pltpu.VMEM((16, WR, 128), BF),
            pltpu.VMEM((WR, 128), BF),
            pltpu.VMEM((HALF, D), BF),
            pltpu.VMEM((1024, D), BF),
            pltpu.VMEM((UNITS, TOK), BF),
            pltpu.VMEM((HALF, 1024), BF),
            pltpu.VMEM((1024, HALF), BF),
            pltpu.VMEM((TOK, TOK), BF),
            pltpu.VMEM((16, WR, 128), BF),
            pltpu.VMEM((8, AG, 128), BF),
            pltpu.VMEM((2, 4, AG, 128), BF),
            pltpu.VMEM((2, 2, 4, BG, 128), BF),
            pltpu.VMEM((BG, 128), BF),
            pltpu.VMEM((BG, 128), BF),
            pltpu.VMEM((WR, 128), BF),
            pltpu.VMEM((WR, 128), BF),
            pltpu.VMEM((2, 2, 2, 256, 1280), BF),
            pltpu.VMEM((2, 2, 256, 1280), BF),
            pltpu.VMEM((2, 2, 2, 32, 1280), BF),
            pltpu.VMEM((2, 2, 2, 64, 1280), BF),
            pltpu.VMEM((2, 64, 1280), BF),
            pltpu.VMEM((2, 64, 1280), BF),
            pltpu.VMEM((2, HALF, TOK), BF),
            pltpu.SemaphoreType.DMA((NSEM,)),
            pltpu.SemaphoreType.DMA((NSEM,)),
            pltpu.SemaphoreType.DMA((8,)),
        ],
        compiler_params=pltpu.CompilerParams(
            collective_id=0, has_side_effects=True, vmem_limit_bytes=62 << 20
        ),
        cost_estimate=pl.CostEstimate(flops=25_000_000_000, bytes_accessed=10_000_000, transcendentals=2_000_000),
    )(gate_t, up_t, down_codes, down_scales, cotangent)

    def whole(rows, cols):
        return pl.BlockSpec((rows, cols), lambda i: (0, 0))

    part = pl.BlockSpec((320, TOK), lambda i: (i, 0))
    gate_grad, up_grad, layer_out, weight_grad = pl.pallas_call(
        last_kernel,
        grid=(5,),
        out_shape=(
            jax.ShapeDtypeStruct((UNITS, TOK), BF),
            jax.ShapeDtypeStruct((UNITS, TOK), BF),
            jax.ShapeDtypeStruct((64, D), BF),
            jax.ShapeDtypeStruct((50, D), F32),
        ),
        in_specs=[part, part, part, whole(64, D), whole(WR, 128)],
        out_specs=(part, part, whole(64, D), whole(50, D)),
        compiler_params=pltpu.CompilerParams(vmem_limit_bytes=62 << 20),
        cost_estimate=pl.CostEstimate(flops=20_000_000, bytes_accessed=10_000_000, transcendentals=1_000_000),
    )(dhid, gate_t, up_t, out, total)
    return layer_out, gate_grad.T, up_grad.T, weight_grad


def solution(mesh):
    return jax.shard_map(
        body,
        mesh=mesh,
        in_specs=(
            P("dp", "tensor"),
            P("dp", "tensor"),
            P(("tensor", "dp"), None),
            P(("tensor", "dp"), None),
            P(("dp", "tensor"), None),
        ),
        out_specs=(
            P(("dp", "tensor"), None),
            P("dp", "tensor"),
            P("dp", "tensor"),
            P(("tensor", "dp"), None),
        ),
        check_vma=False,
    )
```

```python
import jax
import jax.numpy as jnp
from jax import lax
from jax.experimental import pallas as pl
from jax.experimental.pallas import tpu as pltpu
from jax.sharding import PartitionSpec as P

MESH = pl.DeviceIdType.MESH
BF = jnp.bfloat16
F32 = jnp.float32
D = 2560
TOK = 512
UNITS = 1600
HALF = 800
WR = 1008
AR, BR = 576, 432
AG, BG = 480, 528
NSEM = 160
LIMIT = 400 << 17
PART = 160
SCALE = float(16384) ** -0.5
ORDER = (4, 3, -3, 2, -2, 1, -1, 0)


def dot(a, b):
    return jnp.dot(a, b, preferred_element_type=F32)


def dot_nt(a, b):
    return lax.dot_general(a, b, (((1,), (1,)), ((), ())), preferred_element_type=F32)


def kernel(
    gate_hbm, up_hbm, codes_hbm, scales_ref, cot_hbm,
    out_ref, dr, res,
    gate, up, codes_ref, cot_in, wire, stage, w, cot, hid, ht, hs, eye, g, x_in, ra, rb, fq, fb, stage2, stage3,
    lp, lc, ly, lf, lz, lq, dd, ssem, rsem, lsem,
):
    dp, t = lax.axis_index("dp"), lax.axis_index("tensor")
    x, z, y, c = dp // 8, dp % 8, t // 2, t % 2
    half = x // 2
    xb = x % 2
    is_r = c == half
    not_r = c != half
    vb = jnp.where(is_r, xb, 1 - xb)
    zdev = {1: (8 * x + (z + 1) % 8, t), -1: (8 * x + (z + 7) % 8, t)}
    ydev = {1: (dp, 2 * ((y + 1) % 4) + c), -1: (dp, 2 * ((y + 3) % 4) + c)}
    core = (dp, 2 * y + 1 - c)
    qdev = (8 * (x + 1 - 2 * xb) + z, t)
    pdp = 8 * (3 - x) + z
    psame = (pdp, t)
    pother = (pdp, 2 * y + 1 - c)
    pcore = ((pdp, 2 * y), (pdp, 2 * y + 1))

    count = [0]
    index = {}

    def rc(src, dst, dev):
        i = count[0]
        count[0] += 1
        cp = pltpu.make_async_remote_copy(
            src_ref=src, dst_ref=dst, send_sem=ssem.at[i], recv_sem=rsem.at[i],
            device_id=dev, device_id_type=MESH,
        )
        index[id(cp)] = i
        return cp

    sent = []

    def start(cp):
        cp.start()
        sent.append(cp)

    load_gate = pltpu.make_async_copy(gate_hbm, gate, lsem.at[0])
    load_up = pltpu.make_async_copy(up_hbm, up, lsem.at[1])
    load_codes = pltpu.make_async_copy(codes_hbm, codes_ref, lsem.at[7])
    load_cot = pltpu.make_async_copy(cot_hbm, cot_in, lsem.at[8])
    load_codes.start()
    load_cot.start()
    load_gate.start()
    load_up.start()

    barrier = pltpu.get_barrier_semaphore()
    everyone = (zdev[1], zdev[-1], ydev[1], ydev[-1], core, qdev, psame, pother)
    for dev in everyone:
        pl.semaphore_signal(barrier, inc=1, device_id=dev, device_id_type=MESH)

    left = []
    scales = scales_ref[...].T
    load_codes.wait()
    for p in range(20):
        scale = scales[:, p // 2 : p // 2 + 1]
        piece = codes_ref[:, 128 * p : 128 * p + 128].astype(F32) * scale
        stage[48 * p : 48 * p + 48, :] = piece[:48].astype(BF)
        left.append(piece[48:50])
    left.append(jnp.zeros((8, 128), F32))
    stage[960:1008, :] = jnp.concatenate(left, axis=0).astype(BF)

    load_cot.wait()
    pl.semaphore_wait(barrier, len(everyone))

    def blk(b, k):
        return 8 * b + lax.rem(z + k + 8, 8)

    rows_a = slice(0, AR)
    rows_b = slice(AR, WR)
    half_a = {1: pl.ds(0, 288), -1: pl.ds(288, 288)}
    half_b = {1: pl.ds(AR, 224), -1: pl.ds(AR + 224, 208)}
    own_slot = 8 * vb + z

    swap_w = [rc(stage.at[rows], wire.at[8 * xb + z, rows], pother) for rows in (rows_b, rows_a)]
    own_w = pltpu.make_async_copy(stage, wire.at[own_slot], lsem.at[2])

    def ring(b, rows, halves):
        return {
            (d, s): rc(
                wire.at[blk(b, -d * (s - 1)), rows if s < 4 else halves[d]],
                wire.at[blk(b, -d * (s - 1)), rows if s < 4 else halves[d]],
                zdev[d],
            )
            for s in (1, 2, 3, 4)
            for d in (1, -1)
        }

    fa = ring(vb, rows_a, half_a)
    fb_own = ring(vb, rows_b, half_b)
    fb_q = ring(1 - vb, rows_b, half_b)
    q_b = rc(wire.at[own_slot, rows_b], wire.at[own_slot, rows_b], qdev)
    q_a = {
        k: rc(wire.at[blk(vb, k), rows_a], wire.at[blk(vb, k), rows_a], qdev)
        for k in (0, 1, -1, 2, -2, 3, -3)
    }
    for d in (1, -1):
        q_a[4, d] = rc(wire.at[blk(vb, 4), half_a[d]], wire.at[blk(vb, 4), half_a[d]], qdev)

    begin_b = (q_b, fb_own[1, 1], fb_own[-1, 1])
    begin_a = (fa[1, 1], fa[-1, 1], q_a[0])

    def from_stage(cp, rows, dev):
        i = index[id(cp)]
        pltpu.make_async_remote_copy(
            src_ref=stage.at[rows], dst_ref=wire.at[own_slot, rows], send_sem=ssem.at[i], recv_sem=rsem.at[i],
            device_id=dev, device_id_type=MESH,
        ).start()

    sent.extend((q_b, fa[1, 1], fa[-1, 1], fb_own[1, 1], fb_own[-1, 1], q_a[0]))

    def ag_a(s):
        for d in (1, -1):
            fa[d, s].wait_recv()
            if s < 4:
                start(fa[d, s + 1])
                start(q_a[-d * s])
            else:
                start(q_a[4, d])

    def ag_b(s, which):
        for d in (1, -1):
            which[d, s].wait_recv()
            if s < 4:
                start(which[d, s + 1])

    def crow(gr, tt):
        return pl.multiple_of(512 * gr + 64 * tt, 32)

    def cblk(gr, yy, off=0, n=64):
        return cot.at[pl.ds(pl.multiple_of(512 * gr + 64 * (2 * yy + c) + off, 32), n)]

    y1, ym1, y2 = (y + 1) % 4, (y + 3) % 4, (y + 2) % 4
    cot_p = {
        o: rc(cot_in.at[pl.ds(o, 32)], cblk(1, y, o, 32), psame) for o in (0, 32)
    }
    own_c = pltpu.make_async_copy(cot_in, cblk(0, y), lsem.at[3])
    cot_y, cot_h, cot_core = {}, {}, {}
    first = {1: 0, -1: 32}
    for gr in (0, 1):
        for d in (1, -1):
            for o in (0, 32):
                mine = cot_in.at[pl.ds(o, 32)] if gr == 0 else cblk(1, y, o, 32)
                cot_y[gr, d, o] = rc(mine, cblk(gr, y, o, 32), ydev[d])
        cot_h[gr, 1] = rc(cblk(gr, ym1, 0, 32), cblk(gr, ym1, 0, 32), ydev[1])
        cot_h[gr, -1] = rc(cblk(gr, y1, 32, 32), cblk(gr, y1, 32, 32), ydev[-1])
        mine = cot_in if gr == 0 else cblk(1, y)
        cot_core[gr, 0] = rc(mine, cblk(gr, y), core)
        cot_core[gr, 1] = rc(cblk(gr, ym1), cblk(gr, ym1), core)
        cot_core[gr, -1] = rc(cblk(gr, y1), cblk(gr, y1), core)
        cot_core[gr, 2] = rc(cblk(gr, y2, 0, 32), cblk(gr, y2, 0, 32), core)
        cot_core[gr, -2] = rc(cblk(gr, y2, 32, 32), cblk(gr, y2, 32, 32), core)

    def cot_begin():
        for o in (0, 1):
            for d in (1, -1):
                start(cot_y[0, d, first[d] if o == 0 else 32 - first[d]])
        start(cot_core[0, 0])

    def cot_partner():
        for o in (0, 32):
            cot_p[o].wait_recv()
        for o in (0, 1):
            for d in (1, -1):
                start(cot_y[1, d, first[d] if o == 0 else 32 - first[d]])
        start(cot_core[1, 0])

    def cot_forward(gr):
        for d in (1, -1):
            cot_y[gr, d, first[d]].wait_recv()
            start(cot_h[gr, d])

    def cot_rest(gr):
        for d in (1, -1):
            cot_y[gr, d, 32 - first[d]].wait_recv()
            start(cot_core[gr, d])

    def cot_last(gr):
        for d in (1, -1):
            cot_h[gr, d].wait_recv()
            start(cot_core[gr, 2 * d])

    def cot_end(gr):
        for k in (0, 1, -1, 2, -2):
            cot_core[gr, k].wait_recv()

    def rows_of(h, b):
        return pl.ds(pl.multiple_of(HALF * h + 400 * b, 16), 400)

    def cols_of(gr):
        return slice(512 * gr, 512 * gr + 512)

    hid_p, hid_core, hid_own = {}, {}, {}
    for h in (0, 1):
        v_to = jnp.where(h == 1 - half, 1 - xb, xb)
        for o in (0, 1):
            b = 1 - v_to if o == 0 else v_to
            hid_p[h, o] = rc(hid.at[rows_of(h, b)], ht.at[rows_of(0, b), cols_of(1)], pcore[h])
    for h in (0, 1):
        whole = hid.at[HALF * h : HALF * h + HALF]
        hid_core[h] = rc(whole, ht.at[:, cols_of(0)], core)
        hid_own[h] = pltpu.make_async_copy(whole, ht.at[:, cols_of(0)], lsem.at[4])

    def hidden_rows(lo, hi):
        @pl.loop(lo, hi)
        def _(i):
            r = pl.ds(pl.multiple_of(32 * i, 32), 32)
            gv = gate[r, :].astype(F32)
            uv = up[r, :].astype(F32)
            hid[r, :] = (gv * jax.nn.sigmoid(gv) * uv).astype(BF)

    def both(fn):
        for h in (0, 1):
            pl.when(c == h)(lambda h=h: fn(h))

    def cot_to_partner():
        for o in (0, 32):
            cot_p[o].start()

    sent.extend(cot_p.values())

    @pl.when(not_r)
    def _():
        for cp in swap_w:
            cp.start()
        cot_to_partner()

    own_c.start()
    cot_begin()

    @pl.when(is_r)
    def _():
        from_stage(q_b, rows_b, qdev)
        for d in (1, -1):
            from_stage(fa[d, 1], rows_a, zdev[d])
        for d in (1, -1):
            from_stage(fb_own[d, 1], rows_b, zdev[d])
        from_stage(q_a[0], rows_a, qdev)
        own_w.start()

    row = lax.broadcasted_iota(jnp.int32, (TOK, TOK), 0)
    lane = lax.broadcasted_iota(jnp.int32, (TOK, TOK), 1)
    eye[...] = jnp.where(row == lane, 1.0, 0.0).astype(BF)

    load_gate.wait()
    load_up.wait()
    hidden_rows(0, 15)

    pl.when(is_r)(cot_to_partner)

    @pl.when(not_r)
    def _():
        for cp, begin in zip(swap_w, (begin_b, begin_a)):
            cp.wait_recv()
            for follow in begin:
                follow.start()

    hidden_rows(15, 50)

    @pl.when(not_r)
    def _():
        for o in (0, 1):
            for h in (0, 1):
                hid_p[h, o].start()

    @pl.when(is_r)
    def _():
        both(lambda h: hid_own[h].start())
        both(lambda h: hid_core[1 - h].start())

    def turn(gr):
        hs[512 * gr : 512 * gr + 512, :] = dot_nt(eye[...], ht[:, cols_of(gr)]).astype(BF)

    def wgrad(b):
        left = [[] for _ in range(8)]
        lhs = ht[pl.ds(pl.multiple_of(400 * b, 16), 400), :]
        for n in range(5):
            acc = dot(lhs, cot[:, 512 * n : 512 * n + 512])
            for i in range(8):
                for j in range(4):
                    p = 4 * n + j
                    col = acc[50 * i : 50 * i + 50, 128 * j : 128 * j + 128]
                    g[8 * b + i, 48 * p : 48 * p + 48, :] = col[:48].astype(BF)
                    left[i].append(col[48:50])
        for i in range(8):
            tail = jnp.concatenate(left[i] + [jnp.zeros((8, 128), F32)], axis=0)
            g[8 * b + i, 960:1008, :] = tail.astype(BF)

    def unpack(b):
        tails = [wire[8 * b + i, 960:1008, :].astype(F32) for i in range(8)]
        for p in range(20):
            rows = []
            for i in range(8):
                rows.append(wire[8 * b + i, 48 * p : 48 * p + 48, :].astype(F32))
                rows.append(tails[i][2 * p : 2 * p + 2])
            w[pl.ds(pl.multiple_of(400 * b, 16), 400), 128 * p : 128 * p + 128] = jnp.concatenate(rows, axis=0).astype(BF)

    cut_a, cut_b = slice(0, AG), slice(AG, WR)
    part_b = {1: pl.ds(AG, 272), -1: pl.ds(AG + 272, 256)}

    def kidx(k):
        return k + 3

    ga = {k: rc(g.at[blk(1 - vb, k), cut_a], x_in.at[kidx(k)], qdev) for k in ORDER}
    ha = {1: pl.ds(0, 240), -1: pl.ds(240, 240)}
    hb = {1: pl.ds(0, 272), -1: pl.ds(272, 256)}
    ra_c, rb_c = {}, {}
    for s in (1, 2, 3, 4):
        for d in (1, -1):
            if s == 1:
                ra_c[d, s] = rc(x_in.at[kidx(4), ha[d]], ra.at[(1 - d) // 2, 0, ha[d]], zdev[d])
            else:
                ra_c[d, s] = rc(x_in.at[kidx(d * (5 - s))], ra.at[(1 - d) // 2, s - 1], zdev[d])
            for bb, b in ((0, vb), (1, 1 - vb)):
                if s == 1:
                    rb_c[bb, d, s] = rc(g.at[blk(b, 4), part_b[d]], rb.at[bb, (1 - d) // 2, 0, hb[d]], zdev[d])
                else:
                    rb_c[bb, d, s] = rc(g.at[blk(b, d * (5 - s)), cut_b], rb.at[bb, (1 - d) // 2, s - 1], zdev[d])
    fin_q = rc(fq, fb, qdev)
    swap_ga = rc(stage2.at[cut_a], stage3.at[cut_a], pother)
    swap_gb = rc(stage2.at[cut_b], stage3.at[cut_b], pother)

    def add_into(dst, *terms):
        n = dst.shape[0]
        step = next(v for v in (176, 160, 136, 128, 120, 32, 16) if n % v == 0 and v % 16 == 0)

        @pl.loop(0, n // step)
        def _(i):
            r = pl.ds(pl.multiple_of(i * step, 16), step)
            v = dst[r, :].astype(F32)
            for term in terms:
                v = v + term[r, :].astype(F32)
            dst[r, :] = v.astype(dst.dtype)

    def rs_begin(bb):
        for d in (1, -1):
            start(rb_c[bb, d, 1])
        if bb == 1:
            start(ga[4])

    def rs_x(k):
        ga[k].wait_recv()
        add_into(x_in.at[kidx(k)], g.at[blk(vb, k), cut_a])

    def rs_first():
        rs_x(4)
        for d in (1, -1):
            start(ra_c[d, 1])

    def rs_a(s, d):
        k = d * (5 - s)
        rs_x(k)
        ra_c[d, s - 1].wait_recv()
        rows = ha[d] if s == 2 else pl.ds(0, AG)
        add_into(x_in.at[kidx(k), rows], ra.at[(1 - d) // 2, s - 2, rows])
        start(ra_c[d, s])

    def rs_b(bb, s):
        b = 1 - vb if bb == 1 else vb
        for d in (1, -1):
            k = d * (5 - s)
            rb_c[bb, d, s - 1].wait_recv()
            if s == 2:
                dst, src = g.at[blk(b, k), part_b[d]], rb.at[bb, (1 - d) // 2, 0, hb[d]]
            else:
                dst, src = g.at[blk(b, k), cut_b], rb.at[bb, (1 - d) // 2, s - 2]
            add_into(dst, src)
            start(rb_c[bb, d, s])

    def rs_b_other():
        for d in (1, -1):
            rb_c[1, d, 4].wait_recv()
        fq[...] = (
            g[blk(1 - vb, 0), cut_b, :].astype(F32)
            + rb[1, 0, 3].astype(F32)
            + rb[1, 1, 3].astype(F32)
        ).astype(BF)
        start(fin_q)

    def swap_out(rows, cp, total):
        res[rows, :] = total

        @pl.when(not_r)
        def _():
            stage2[rows, :] = total.astype(BF)
            cp.start()

    def rs_b_end():
        for d in (1, -1):
            rb_c[0, d, 4].wait_recv()
        part = g[blk(vb, 0), cut_b, :].astype(F32) + rb[0, 0, 3].astype(F32) + rb[0, 1, 3].astype(F32)
        fin_q.wait_recv()
        swap_out(cut_b, swap_gb, part + fb[...].astype(F32))

    def rs_a_end():
        for d in (1, -1):
            ra_c[d, 4].wait_recv()
        total = x_in[kidx(0)].astype(F32) + ra[0, 3].astype(F32) + ra[1, 3].astype(F32)
        swap_out(cut_a, swap_ga, total)

    def rs_end():
        @pl.when(not_r)
        def _():
            swap_gb.wait_recv()
            res[cut_b, :] = stage3[cut_b, :].astype(F32)
            swap_ga.wait_recv()
            res[cut_a, :] = stage3[cut_a, :].astype(F32)
            swap_ga.wait_send()
            swap_gb.wait_send()

    def layer(gr, ch):
        @pl.loop(0, 5)
        def _(n):
            off = pl.multiple_of(256 * n, 256)
            acc = dot(hs[512 * gr : 512 * gr + 512, :], w[:, pl.ds(pl.multiple_of(1280 * ch + off, 256), 256)])
            for tt in range(8):
                r = 64 * (tt // 2)
                lp[gr, ch, tt % 2, r : r + 64, pl.ds(off, 256)] = acc[64 * tt : 64 * tt + 64].astype(BF)

    l_core, l_y1, l_y2, l_p = {}, {}, {}, {}

    def yrow(yy, off=0, n=64):
        return pl.ds(pl.multiple_of(64 * yy + off, 32), n)

    for gr in (1, 0):
        for ch in (0, 1):
            l_core[gr, ch] = rc(lp.at[gr, ch, 1 - c], lc.at[gr, ch], core)
            for d in (1, -1):
                o = 0 if d == 1 else 32
                l_y1[gr, ch, d] = rc(lc.at[gr, ch, yrow(y2, o, 32)], ly.at[gr, ch, (1 - d) // 2], ydev[d])
                to = y1 if d == 1 else ym1
                l_y2[gr, ch, d] = rc(lc.at[gr, ch, yrow(to)], lf.at[gr, ch, (1 - d) // 2], ydev[d])
    for ch in (0, 1):
        l_p[ch] = rc(lz.at[ch], lq.at[ch], psame)

    def layer_core(gr, ch):
        l_core[gr, ch].wait_recv()
        add_into(lc.at[gr, ch], lp.at[gr, ch, c])
        for d in (1, -1):
            start(l_y1[gr, ch, d])

    def layer_y(gr, ch):
        for d in (1, -1):
            l_y1[gr, ch, d].wait_recv()
            o = 0 if d == 1 else 32
            to = y1 if d == 1 else ym1
            add_into(lc.at[gr, ch, yrow(to, o, 32)], ly.at[gr, ch, (1 - d) // 2])
            start(l_y2[gr, ch, d])

    def layer_end(gr, ch):
        for d in (1, -1):
            l_y2[gr, ch, d].wait_recv()
        total = lc[gr, ch, yrow(y), :].astype(F32) + lf[gr, ch, 0].astype(F32) + lf[gr, ch, 1].astype(F32)
        if gr == 1:
            lz[ch] = total.astype(BF)
            start(l_p[ch])
        else:
            l_p[ch].wait_recv()
            out_ref[:, 1280 * ch : 1280 * ch + 1280] = (total + lq[ch].astype(F32)).astype(BF)

    def half_of(o):
        return vb if o == 0 else 1 - vb

    def rows_at(q):
        return pl.ds(pl.multiple_of(400 * q, 16), 400)

    def drows(h, o):
        return pl.ds(pl.multiple_of(HALF * h + 400 * half_of(o), 16), 400)

    d_p, d_core, d_own = {}, {}, {}
    for h in (0, 1):
        for q in (0, 1):
            src = dd.at[1, rows_at(half_of(q))]
            d_p["same", h, q] = rc(src, dr.at[drows(h, q)], psame)
            d_p["other", h, q] = rc(src, dr.at[drows(h, q)], pother)
            src = dd.at[0, rows_at(half_of(q))]
            d_core[h, q] = rc(src, dr.at[drows(h, q)], core)
            d_own[h, q] = pltpu.make_async_copy(src, dr.at[drows(h, q)], lsem.at[5 + q])

    def dhidden(gr, o):
        r = rows_at(half_of(o))
        dd[gr, r, :] = dot_nt(w[r, :], cot[512 * gr : 512 * gr + 512, :]).astype(BF)

    def d_send_p(q):
        @pl.when(is_r)
        def _():
            both(lambda h: d_p["same", h, q].start())

        @pl.when(not_r)
        def _():
            both(lambda h: d_p["other", h, q].start())

    def d_send_core(q):
        @pl.when(is_r)
        def _():
            both(lambda h: d_own[h, q].start())

        @pl.when(not_r)
        def _():
            both(lambda h: d_core[h, q].start())

    def d_recv(q):
        @pl.when(is_r)
        def _():
            both(lambda h: d_own[h, q].wait())
            both(lambda h: d_core[1 - h, q].wait_recv())

        @pl.when(not_r)
        def _():
            def arrive(h):
                d_p["same", h, q].wait_recv()
                d_p["other", 1 - h, q].wait_recv()

            both(arrive)

    def d_sent():
        for q in (0, 1):
            @pl.when(is_r)
            def _():
                both(lambda h: d_p["same", h, q].wait_send())

            @pl.when(not_r)
            def _():
                both(lambda h: d_p["other", h, q].wait_send())
                both(lambda h: d_core[h, q].wait_send())

    q_b.wait_recv()
    for d in (1, -1):
        start(fb_q[d, 1])
    ag_a(1)
    cot_forward(0)

    @pl.when(is_r)
    def _():
        both(lambda h: hid_own[h].wait())
        own_w.wait()

    @pl.when(not_r)
    def _():
        both(lambda h: hid_core[h].wait_recv())

    turn(0)
    ag_b(1, fb_own)
    cot_partner()
    ag_b(1, fb_q)
    cot_rest(0)
    cot_last(0)
    ag_a(2)
    cot_forward(1)
    ag_b(2, fb_own)
    ag_b(2, fb_q)
    cot_rest(1)
    ag_a(3)
    cot_last(1)
    ag_b(3, fb_own)
    cot_end(0)
    cot_end(1)
    own_c.wait()
    both(lambda h: hid_p[h, 0].wait_recv())
    wgrad(1 - vb)
    rs_begin(1)
    ag_a(4)
    ag_b(3, fb_q)
    for k in ORDER[1:]:
        start(ga[k])
    both(lambda h: hid_p[h, 1].wait_recv())
    wgrad(vb)
    rs_begin(0)
    ag_b(4, fb_own)
    unpack(vb)
    dhidden(1, 0)
    d_send_p(0)
    rs_b(1, 2)
    ag_b(4, fb_q)
    rs_first()
    turn(1)
    for k in (0, 1, -1, 2, -2, 3, -3):
        q_a[k].wait_recv()
    for d in (1, -1):
        q_a[4, d].wait_recv()
    unpack(1 - vb)
    layer(1, 0)
    start(l_core[1, 0])
    rs_b(0, 2)
    layer_core(1, 0)
    rs_a(2, 1)
    dhidden(1, 1)
    d_send_p(1)
    rs_b(1, 3)
    rs_a(2, -1)
    layer(1, 1)
    start(l_core[1, 1])
    rs_b(0, 3)
    layer_y(1, 0)
    dhidden(0, 0)
    d_send_core(0)
    rs_a(3, 1)
    layer_core(1, 1)
    rs_b(1, 4)
    rs_a(3, -1)
    dhidden(0, 1)
    d_send_core(1)
    layer(0, 0)
    start(l_core[0, 0])
    rs_b(0, 4)
    layer_y(1, 1)
    rs_a(4, 1)
    layer(0, 1)
    start(l_core[0, 1])
    layer_core(0, 0)
    rs_a(4, -1)
    layer_end(1, 0)
    rs_b_other()
    layer_core(0, 1)
    layer_y(0, 0)
    layer_end(1, 1)
    rs_x(0)
    layer_y(0, 1)
    for q in (0, 1):
        d_recv(q)
    rs_b_end()
    rs_a_end()
    layer_end(0, 0)
    layer_end(0, 1)
    rs_end()

    for cp in sent:
        cp.wait_send()

    @pl.when(not_r)
    def _():
        for cp in swap_w:
            cp.wait_send()
        for o in (0, 1):
            for h in (0, 1):
                hid_p[h, o].wait_send()

    @pl.when(is_r)
    def _():
        both(lambda h: hid_core[1 - h].wait_send())

    d_sent()


def last_kernel(dr, gate, up, out, res, gg_hbm, ug_hbm, lo_hbm, wg_hbm, gg, ug, wg, osem):
    def part(i):
        return pl.ds(PART * i, PART)

    n = UNITS // PART
    saves = [pltpu.make_async_copy(out, lo_hbm, osem.at[2 * n])]
    saves[0].start()
    for p in range(20):
        cols = slice(128 * p, 128 * p + 128)
        wg[0:48, cols] = res[48 * p : 48 * p + 48, :] * SCALE
        wg[48:50, cols] = res[960 + 2 * p : 962 + 2 * p, :] * SCALE
    saves.append(pltpu.make_async_copy(wg, wg_hbm, osem.at[2 * n + 1]))
    saves[1].start()
    for i in range(n):
        @pl.loop(0, PART // 16)
        def _(k):
            r = pl.ds(pl.multiple_of(PART * i + 16 * k, 16), 16)
            dv = dr[r, :].astype(F32)
            gv = gate[r, :].astype(F32)
            uv = up[r, :].astype(F32)
            sv = jax.nn.sigmoid(gv)
            gg[r, :] = (dv * uv * sv * (1.0 + gv * (1.0 - sv))).astype(BF)
            ug[r, :] = (dv * (gv * sv)).astype(BF)

        for j, (src, dst) in enumerate(((gg, gg_hbm), (ug, ug_hbm))):
            cp = pltpu.make_async_copy(src.at[part(i)], dst.at[part(i)], osem.at[2 * i + j])
            cp.start()
            saves.append(cp)
    for cp in saves:
        cp.wait()


def body(gate_pre, up_pre, down_codes, down_scales, cotangent):
    vmem = pl.BlockSpec(memory_space=pltpu.VMEM)
    anywhere = pl.BlockSpec(memory_space=pl.ANY)
    gate_t, up_t = gate_pre.T, up_pre.T
    out, dhid, total = pl.pallas_call(
        kernel,
        out_shape=(
            jax.ShapeDtypeStruct((64, D), BF),
            jax.ShapeDtypeStruct((UNITS, TOK), BF),
            jax.ShapeDtypeStruct((WR, 128), F32),
        ),
        in_specs=[anywhere, anywhere, anywhere, vmem, anywhere],
        out_specs=(vmem,) * 3,
        scratch_shapes=[
            pltpu.VMEM((UNITS, TOK), BF),
            pltpu.VMEM((UNITS, TOK), BF),
            pltpu.VMEM((50, D), BF),
            pltpu.VMEM((64, D), BF),
            pltpu.VMEM((16, WR, 128), BF),
            pltpu.VMEM((WR, 128), BF),
            pltpu.VMEM((HALF, D), BF),
            pltpu.VMEM((1024, D), BF),
            pltpu.VMEM((UNITS, TOK), BF),
            pltpu.VMEM((HALF, 1024), BF),
            pltpu.VMEM((1024, HALF), BF),
            pltpu.VMEM((TOK, TOK), BF),
            pltpu.VMEM((16, WR, 128), BF),
            pltpu.VMEM((8, AG, 128), BF),
            pltpu.VMEM((2, 4, AG, 128), BF),
            pltpu.VMEM((2, 2, 4, BG, 128), BF),
            pltpu.VMEM((BG, 128), BF),
            pltpu.VMEM((BG, 128), BF),
            pltpu.VMEM((WR, 128), BF),
            pltpu.VMEM((WR, 128), BF),
            pltpu.VMEM((2, 2, 2, 256, 1280), BF),
            pltpu.VMEM((2, 2, 256, 1280), BF),
            pltpu.VMEM((2, 2, 2, 32, 1280), BF),
            pltpu.VMEM((2, 2, 2, 64, 1280), BF),
            pltpu.VMEM((2, 64, 1280), BF),
            pltpu.VMEM((2, 64, 1280), BF),
            pltpu.VMEM((2, HALF, TOK), BF),
            pltpu.SemaphoreType.DMA((NSEM,)),
            pltpu.SemaphoreType.DMA((NSEM,)),
            pltpu.SemaphoreType.DMA((16,)),
        ],
        compiler_params=pltpu.CompilerParams(
            collective_id=0, has_side_effects=True, vmem_limit_bytes=LIMIT
        ),
        cost_estimate=pl.CostEstimate(flops=25_000_000_000, bytes_accessed=10_000_000, transcendentals=2_000_000),
    )(gate_t, up_t, down_codes, down_scales.T, cotangent)

    gate_grad, up_grad, layer_out, weight_grad = pl.pallas_call(
        last_kernel,
        out_shape=(
            jax.ShapeDtypeStruct((UNITS, TOK), BF),
            jax.ShapeDtypeStruct((UNITS, TOK), BF),
            jax.ShapeDtypeStruct((64, D), BF),
            jax.ShapeDtypeStruct((50, D), F32),
        ),
        in_specs=[vmem] * 5,
        out_specs=(anywhere,) * 4,
        scratch_shapes=[
            pltpu.VMEM((UNITS, TOK), BF),
            pltpu.VMEM((UNITS, TOK), BF),
            pltpu.VMEM((50, D), F32),
            pltpu.SemaphoreType.DMA((2 * UNITS // PART + 2,)),
        ],
        compiler_params=pltpu.CompilerParams(vmem_limit_bytes=24 << 20),
        cost_estimate=pl.CostEstimate(flops=20_000_000, bytes_accessed=10_000_000, transcendentals=1_000_000),
    )(dhid, gate_t, up_t, out, total)
    return layer_out, gate_grad.T, up_grad.T, weight_grad


def solution(mesh):
    return jax.shard_map(
        body,
        mesh=mesh,
        in_specs=(
            P("dp", "tensor"),
            P("dp", "tensor"),
            P(("tensor", "dp"), None),
            P(("tensor", "dp"), None),
            P(("dp", "tensor"), None),
        ),
        out_specs=(
            P(("dp", "tensor"), None),
            P("dp", "tensor"),
            P("dp", "tensor"),
            P(("tensor", "dp"), None),
        ),
        check_vma=False,
    )
```

```python
import jax
import jax.numpy as jnp
from jax import lax
from jax.experimental import pallas as pl
from jax.experimental.pallas import tpu as pltpu
from jax.sharding import PartitionSpec as P

MESH = pl.DeviceIdType.MESH
BF = jnp.bfloat16
F32 = jnp.float32
D = 2560
TOK = 512
UNITS = 1600
HALF = 800
WR = 1008
AR, BR = 576, 432
AG, BG = 480, 528
NSEM = 160
LIMIT = 400 << 17
PART = 160
SCALE = float(16384) ** -0.5
ORDER = (4, 3, -3, 2, -2, 1, -1, 0)


def dot(a, b):
    return jnp.dot(a, b, preferred_element_type=F32)


def dot_nt(a, b):
    return lax.dot_general(a, b, (((1,), (1,)), ((), ())), preferred_element_type=F32)


def kernel(
    gate_hbm, up_hbm, codes_hbm, scales_ref, cot_hbm,
    out_ref, dr, res,
    gate, up, codes_ref, cot_in, wire, stage, w, cot, hid, ht, hs, eye, g, x_in, ra, rb, fq, fb, stage2, stage3,
    lp, lc, ly, lf, lz, lq, dd, ssem, rsem, lsem,
):
    dp, t = lax.axis_index("dp"), lax.axis_index("tensor")
    x, z, y, c = dp // 8, dp % 8, t // 2, t % 2
    half = x // 2
    xb = x % 2
    is_r = c == half
    not_r = c != half
    vb = jnp.where(is_r, xb, 1 - xb)
    zdev = {1: (8 * x + (z + 1) % 8, t), -1: (8 * x + (z + 7) % 8, t)}
    ydev = {1: (dp, 2 * ((y + 1) % 4) + c), -1: (dp, 2 * ((y + 3) % 4) + c)}
    core = (dp, 2 * y + 1 - c)
    qdev = (8 * (x + 1 - 2 * xb) + z, t)
    pdp = 8 * (3 - x) + z
    psame = (pdp, t)
    pother = (pdp, 2 * y + 1 - c)
    pcore = ((pdp, 2 * y), (pdp, 2 * y + 1))

    count = [0]
    index = {}

    def rc(src, dst, dev):
        i = count[0]
        count[0] += 1
        cp = pltpu.make_async_remote_copy(
            src_ref=src, dst_ref=dst, send_sem=ssem.at[i], recv_sem=rsem.at[i],
            device_id=dev, device_id_type=MESH,
        )
        index[id(cp)] = i
        return cp

    sent = []

    def start(cp):
        cp.start()
        sent.append(cp)

    load_gate = pltpu.make_async_copy(gate_hbm, gate, lsem.at[0])
    load_up = pltpu.make_async_copy(up_hbm, up, lsem.at[1])
    load_codes = pltpu.make_async_copy(codes_hbm, codes_ref, lsem.at[7])
    load_cot = pltpu.make_async_copy(cot_hbm, cot_in, lsem.at[8])
    load_codes.start()
    load_cot.start()
    load_gate.start()
    load_up.start()

    barrier = pltpu.get_barrier_semaphore()
    everyone = (zdev[1], zdev[-1], ydev[1], ydev[-1], core, qdev, psame, pother)
    for dev in everyone:
        pl.semaphore_signal(barrier, inc=1, device_id=dev, device_id_type=MESH)

    left = []
    scales = scales_ref[...].T
    load_codes.wait()
    for p in range(20):
        scale = scales[:, p // 2 : p // 2 + 1]
        piece = codes_ref[:, 128 * p : 128 * p + 128].astype(F32) * scale
        stage[48 * p : 48 * p + 48, :] = piece[:48].astype(BF)
        left.append(piece[48:50])
    left.append(jnp.zeros((8, 128), F32))
    stage[960:1008, :] = jnp.concatenate(left, axis=0).astype(BF)

    load_cot.wait()
    pl.semaphore_wait(barrier, len(everyone))

    def blk(b, k):
        return 8 * b + lax.rem(z + k + 8, 8)

    rows_a = slice(0, AR)
    rows_b = slice(AR, WR)
    half_a = {1: pl.ds(0, 288), -1: pl.ds(288, 288)}
    half_b = {1: pl.ds(AR, 224), -1: pl.ds(AR + 224, 208)}
    own_slot = 8 * vb + z

    swap_w = [rc(stage.at[rows], wire.at[8 * xb + z, rows], pother) for rows in (rows_b, rows_a)]
    own_w = pltpu.make_async_copy(stage, wire.at[own_slot], lsem.at[2])

    def ring(b, rows, halves):
        return {
            (d, s): rc(
                wire.at[blk(b, -d * (s - 1)), rows if s < 4 else halves[d]],
                wire.at[blk(b, -d * (s - 1)), rows if s < 4 else halves[d]],
                zdev[d],
            )
            for s in (1, 2, 3, 4)
            for d in (1, -1)
        }

    fa = ring(vb, rows_a, half_a)
    fb_own = ring(vb, rows_b, half_b)
    fb_q = ring(1 - vb, rows_b, half_b)
    q_b = rc(wire.at[own_slot, rows_b], wire.at[own_slot, rows_b], qdev)
    q_a = {
        k: rc(wire.at[blk(vb, k), rows_a], wire.at[blk(vb, k), rows_a], qdev)
        for k in (0, 1, -1, 2, -2, 3, -3)
    }
    for d in (1, -1):
        q_a[4, d] = rc(wire.at[blk(vb, 4), half_a[d]], wire.at[blk(vb, 4), half_a[d]], qdev)

    begin_b = (q_b, fb_own[1, 1], fb_own[-1, 1])
    begin_a = (fa[1, 1], fa[-1, 1], q_a[0])

    def from_stage(cp, rows, dev):
        i = index[id(cp)]
        pltpu.make_async_remote_copy(
            src_ref=stage.at[rows], dst_ref=wire.at[own_slot, rows], send_sem=ssem.at[i], recv_sem=rsem.at[i],
            device_id=dev, device_id_type=MESH,
        ).start()

    sent.extend((q_b, fa[1, 1], fa[-1, 1], fb_own[1, 1], fb_own[-1, 1], q_a[0]))

    def ag_a(s):
        for d in (1, -1):
            fa[d, s].wait_recv()
            if s < 4:
                start(fa[d, s + 1])
                start(q_a[-d * s])
            else:
                start(q_a[4, d])

    def ag_b(s, which):
        for d in (1, -1):
            which[d, s].wait_recv()
            if s < 4:
                start(which[d, s + 1])

    def crow(gr, tt):
        return pl.multiple_of(512 * gr + 64 * tt, 32)

    def cblk(gr, yy, off=0, n=64):
        return cot.at[pl.ds(pl.multiple_of(512 * gr + 64 * (2 * yy + c) + off, 32), n)]

    y1, ym1, y2 = (y + 1) % 4, (y + 3) % 4, (y + 2) % 4
    cot_p = {
        o: rc(cot_in.at[pl.ds(o, 32)], cblk(1, y, o, 32), psame) for o in (0, 32)
    }
    own_c = pltpu.make_async_copy(cot_in, cblk(0, y), lsem.at[3])
    cot_y, cot_h, cot_core = {}, {}, {}
    first = {1: 0, -1: 32}
    for gr in (0, 1):
        for d in (1, -1):
            for o in (0, 32):
                mine = cot_in.at[pl.ds(o, 32)] if gr == 0 else cblk(1, y, o, 32)
                cot_y[gr, d, o] = rc(mine, cblk(gr, y, o, 32), ydev[d])
        cot_h[gr, 1] = rc(cblk(gr, ym1, 0, 32), cblk(gr, ym1, 0, 32), ydev[1])
        cot_h[gr, -1] = rc(cblk(gr, y1, 32, 32), cblk(gr, y1, 32, 32), ydev[-1])
        mine = cot_in if gr == 0 else cblk(1, y)
        cot_core[gr, 0] = rc(mine, cblk(gr, y), core)
        cot_core[gr, 1] = rc(cblk(gr, ym1), cblk(gr, ym1), core)
        cot_core[gr, -1] = rc(cblk(gr, y1), cblk(gr, y1), core)
        cot_core[gr, 2] = rc(cblk(gr, y2, 0, 32), cblk(gr, y2, 0, 32), core)
        cot_core[gr, -2] = rc(cblk(gr, y2, 32, 32), cblk(gr, y2, 32, 32), core)

    def cot_begin():
        for o in (0, 1):
            for d in (1, -1):
                start(cot_y[0, d, first[d] if o == 0 else 32 - first[d]])
        start(cot_core[0, 0])

    def cot_partner():
        for o in (0, 32):
            cot_p[o].wait_recv()
        for o in (0, 1):
            for d in (1, -1):
                start(cot_y[1, d, first[d] if o == 0 else 32 - first[d]])
        start(cot_core[1, 0])

    def cot_forward(gr):
        for d in (1, -1):
            cot_y[gr, d, first[d]].wait_recv()
            start(cot_h[gr, d])

    def cot_rest(gr):
        for d in (1, -1):
            cot_y[gr, d, 32 - first[d]].wait_recv()
            start(cot_core[gr, d])

    def cot_last(gr):
        for d in (1, -1):
            cot_h[gr, d].wait_recv()
            start(cot_core[gr, 2 * d])

    def cot_end(gr):
        for k in (0, 1, -1, 2, -2):
            cot_core[gr, k].wait_recv()

    def rows_of(h, b):
        return pl.ds(pl.multiple_of(HALF * h + 400 * b, 16), 400)

    def cols_of(gr):
        return slice(512 * gr, 512 * gr + 512)

    hid_p, hid_core, hid_own = {}, {}, {}
    for h in (0, 1):
        v_to = jnp.where(h == 1 - half, 1 - xb, xb)
        for o in (0, 1):
            b = 1 - v_to if o == 0 else v_to
            hid_p[h, o] = rc(hid.at[rows_of(h, b)], ht.at[rows_of(0, b), cols_of(1)], pcore[h])
    for h in (0, 1):
        whole = hid.at[HALF * h : HALF * h + HALF]
        hid_core[h] = rc(whole, ht.at[:, cols_of(0)], core)
        hid_own[h] = pltpu.make_async_copy(whole, ht.at[:, cols_of(0)], lsem.at[4])

    def hidden_rows(lo, hi):
        @pl.loop(lo, hi)
        def _(i):
            r = pl.ds(pl.multiple_of(32 * i, 32), 32)
            gv = gate[r, :].astype(F32)
            uv = up[r, :].astype(F32)
            hid[r, :] = (gv * jax.nn.sigmoid(gv) * uv).astype(BF)

    def both(fn):
        for h in (0, 1):
            pl.when(c == h)(lambda h=h: fn(h))

    def cot_to_partner():
        for o in (0, 32):
            cot_p[o].start()

    sent.extend(cot_p.values())

    @pl.when(not_r)
    def _():
        for cp in swap_w:
            cp.start()
        cot_to_partner()

    own_c.start()
    cot_begin()

    @pl.when(is_r)
    def _():
        from_stage(q_b, rows_b, qdev)
        for d in (1, -1):
            from_stage(fa[d, 1], rows_a, zdev[d])
        for d in (1, -1):
            from_stage(fb_own[d, 1], rows_b, zdev[d])
        from_stage(q_a[0], rows_a, qdev)
        own_w.start()

    row = lax.broadcasted_iota(jnp.int32, (TOK, TOK), 0)
    lane = lax.broadcasted_iota(jnp.int32, (TOK, TOK), 1)
    eye[...] = jnp.where(row == lane, 1.0, 0.0).astype(BF)

    load_gate.wait()
    load_up.wait()
    hidden_rows(0, 15)

    pl.when(is_r)(cot_to_partner)

    @pl.when(not_r)
    def _():
        for cp, begin in zip(swap_w, (begin_b, begin_a)):
            cp.wait_recv()
            for follow in begin:
                follow.start()

    hidden_rows(15, 50)

    @pl.when(not_r)
    def _():
        for o in (0, 1):
            for h in (0, 1):
                hid_p[h, o].start()

    @pl.when(is_r)
    def _():
        both(lambda h: hid_own[h].start())
        both(lambda h: hid_core[1 - h].start())

    def turn(gr):
        hs[512 * gr : 512 * gr + 512, :] = dot_nt(eye[...], ht[:, cols_of(gr)]).astype(BF)

    def wgrad(b):
        left = [[] for _ in range(8)]
        lhs = ht[pl.ds(pl.multiple_of(400 * b, 16), 400), :]
        for n in range(5):
            acc = dot(lhs, cot[:, 512 * n : 512 * n + 512])
            for i in range(8):
                for j in range(4):
                    p = 4 * n + j
                    col = acc[50 * i : 50 * i + 50, 128 * j : 128 * j + 128]
                    g[8 * b + i, 48 * p : 48 * p + 48, :] = col[:48].astype(BF)
                    left[i].append(col[48:50])
        for i in range(8):
            tail = jnp.concatenate(left[i] + [jnp.zeros((8, 128), F32)], axis=0)
            g[8 * b + i, 960:1008, :] = tail.astype(BF)

    def unpack(b):
        tails = [wire[8 * b + i, 960:1008, :].astype(F32) for i in range(8)]
        for p in range(20):
            rows = []
            for i in range(8):
                rows.append(wire[8 * b + i, 48 * p : 48 * p + 48, :].astype(F32))
                rows.append(tails[i][2 * p : 2 * p + 2])
            w[pl.ds(pl.multiple_of(400 * b, 16), 400), 128 * p : 128 * p + 128] = jnp.concatenate(rows, axis=0).astype(BF)

    cut_a, cut_b = slice(0, AG), slice(AG, WR)
    part_b = {1: pl.ds(AG, 272), -1: pl.ds(AG + 272, 256)}

    def kidx(k):
        return k + 3

    ga = {k: rc(g.at[blk(1 - vb, k), cut_a], x_in.at[kidx(k)], qdev) for k in ORDER}
    ha = {1: pl.ds(0, 240), -1: pl.ds(240, 240)}
    hb = {1: pl.ds(0, 272), -1: pl.ds(272, 256)}
    ra_c, rb_c = {}, {}
    for s in (1, 2, 3, 4):
        for d in (1, -1):
            if s == 1:
                ra_c[d, s] = rc(x_in.at[kidx(4), ha[d]], ra.at[(1 - d) // 2, 0, ha[d]], zdev[d])
            else:
                ra_c[d, s] = rc(x_in.at[kidx(d * (5 - s))], ra.at[(1 - d) // 2, s - 1], zdev[d])
            for bb, b in ((0, vb), (1, 1 - vb)):
                if s == 1:
                    rb_c[bb, d, s] = rc(g.at[blk(b, 4), part_b[d]], rb.at[bb, (1 - d) // 2, 0, hb[d]], zdev[d])
                else:
                    rb_c[bb, d, s] = rc(g.at[blk(b, d * (5 - s)), cut_b], rb.at[bb, (1 - d) // 2, s - 1], zdev[d])
    fin_q = rc(fq, fb, qdev)
    swap_ga = rc(stage2.at[cut_a], stage3.at[cut_a], pother)
    swap_gb = rc(stage2.at[cut_b], stage3.at[cut_b], pother)

    def add_into(dst, *terms):
        n = dst.shape[0]
        step = next(v for v in (176, 160, 136, 128, 120, 32, 16) if n % v == 0 and v % 16 == 0)

        @pl.loop(0, n // step)
        def _(i):
            r = pl.ds(pl.multiple_of(i * step, 16), step)
            v = dst[r, :].astype(F32)
            for term in terms:
                v = v + term[r, :].astype(F32)
            dst[r, :] = v.astype(dst.dtype)

    def rs_begin(bb):
        for d in (1, -1):
            start(rb_c[bb, d, 1])
        if bb == 1:
            start(ga[4])

    def rs_x(k):
        ga[k].wait_recv()
        add_into(x_in.at[kidx(k)], g.at[blk(vb, k), cut_a])

    def rs_first():
        rs_x(4)
        for d in (1, -1):
            start(ra_c[d, 1])

    def rs_a(s, d):
        k = d * (5 - s)
        rs_x(k)
        ra_c[d, s - 1].wait_recv()
        rows = ha[d] if s == 2 else pl.ds(0, AG)
        add_into(x_in.at[kidx(k), rows], ra.at[(1 - d) // 2, s - 2, rows])
        start(ra_c[d, s])

    def rs_b(bb, s):
        b = 1 - vb if bb == 1 else vb
        for d in (1, -1):
            k = d * (5 - s)
            rb_c[bb, d, s - 1].wait_recv()
            if s == 2:
                dst, src = g.at[blk(b, k), part_b[d]], rb.at[bb, (1 - d) // 2, 0, hb[d]]
            else:
                dst, src = g.at[blk(b, k), cut_b], rb.at[bb, (1 - d) // 2, s - 2]
            add_into(dst, src)
            start(rb_c[bb, d, s])

    def rs_b_other():
        for d in (1, -1):
            rb_c[1, d, 4].wait_recv()
        fq[...] = (
            g[blk(1 - vb, 0), cut_b, :].astype(F32)
            + rb[1, 0, 3].astype(F32)
            + rb[1, 1, 3].astype(F32)
        ).astype(BF)
        start(fin_q)

    def swap_out(rows, cp, total):
        res[rows, :] = total

        @pl.when(not_r)
        def _():
            stage2[rows, :] = total.astype(BF)
            cp.start()

    def rs_b_end():
        for d in (1, -1):
            rb_c[0, d, 4].wait_recv()
        part = g[blk(vb, 0), cut_b, :].astype(F32) + rb[0, 0, 3].astype(F32) + rb[0, 1, 3].astype(F32)
        fin_q.wait_recv()
        swap_out(cut_b, swap_gb, part + fb[...].astype(F32))

    def rs_a_end():
        for d in (1, -1):
            ra_c[d, 4].wait_recv()
        total = x_in[kidx(0)].astype(F32) + ra[0, 3].astype(F32) + ra[1, 3].astype(F32)
        swap_out(cut_a, swap_ga, total)

    def rs_end():
        @pl.when(not_r)
        def _():
            swap_gb.wait_recv()
            res[cut_b, :] = stage3[cut_b, :].astype(F32)
            swap_ga.wait_recv()
            res[cut_a, :] = stage3[cut_a, :].astype(F32)
            swap_ga.wait_send()
            swap_gb.wait_send()

    def layer(gr, ch, n):
        off = 640 * n
        acc = dot(hs[512 * gr : 512 * gr + 512, :], w[:, 1280 * ch + off : 1280 * ch + off + 640])
        for tt in range(8):
            r = 64 * (tt // 2)
            lp[gr, ch, tt % 2, r : r + 64, off : off + 640] = acc[64 * tt : 64 * tt + 64].astype(BF)
        if n == 1:
            start(l_core[gr, ch])

    l_core, l_y1, l_y2, l_p = {}, {}, {}, {}

    def yrow(yy, off=0, n=64):
        return pl.ds(pl.multiple_of(64 * yy + off, 32), n)

    for gr in (1, 0):
        for ch in (0, 1):
            l_core[gr, ch] = rc(lp.at[gr, ch, 1 - c], lc.at[gr, ch], core)
            for d in (1, -1):
                o = 0 if d == 1 else 32
                l_y1[gr, ch, d] = rc(lc.at[gr, ch, yrow(y2, o, 32)], ly.at[gr, ch, (1 - d) // 2], ydev[d])
                to = y1 if d == 1 else ym1
                l_y2[gr, ch, d] = rc(lc.at[gr, ch, yrow(to)], lf.at[gr, ch, (1 - d) // 2], ydev[d])
    for ch in (0, 1):
        l_p[ch] = rc(lz.at[ch], lq.at[ch], psame)

    def layer_core(gr, ch):
        l_core[gr, ch].wait_recv()
        add_into(lc.at[gr, ch], lp.at[gr, ch, c])
        for d in (1, -1):
            start(l_y1[gr, ch, d])

    def layer_y(gr, ch):
        for d in (1, -1):
            l_y1[gr, ch, d].wait_recv()
            o = 0 if d == 1 else 32
            to = y1 if d == 1 else ym1
            add_into(lc.at[gr, ch, yrow(to, o, 32)], ly.at[gr, ch, (1 - d) // 2])
            start(l_y2[gr, ch, d])

    def layer_end(gr, ch):
        for d in (1, -1):
            l_y2[gr, ch, d].wait_recv()
        total = lc[gr, ch, yrow(y), :].astype(F32) + lf[gr, ch, 0].astype(F32) + lf[gr, ch, 1].astype(F32)
        if gr == 1:
            lz[ch] = total.astype(BF)
            start(l_p[ch])
        else:
            l_p[ch].wait_recv()
            out_ref[:, 1280 * ch : 1280 * ch + 1280] = (total + lq[ch].astype(F32)).astype(BF)

    def half_of(o):
        return vb if o == 0 else 1 - vb

    def rows_at(q):
        return pl.ds(pl.multiple_of(400 * q, 16), 400)

    def drows(h, o):
        return pl.ds(pl.multiple_of(HALF * h + 400 * half_of(o), 16), 400)

    d_p, d_core, d_own = {}, {}, {}
    for h in (0, 1):
        for q in (0, 1):
            src = dd.at[1, rows_at(half_of(q))]
            d_p["same", h, q] = rc(src, dr.at[drows(h, q)], psame)
            d_p["other", h, q] = rc(src, dr.at[drows(h, q)], pother)
            src = dd.at[0, rows_at(half_of(q))]
            d_core[h, q] = rc(src, dr.at[drows(h, q)], core)
            d_own[h, q] = pltpu.make_async_copy(src, dr.at[drows(h, q)], lsem.at[5 + q])

    def dhidden(gr, o):
        r = rows_at(half_of(o))
        dd[gr, r, :] = dot_nt(w[r, :], cot[512 * gr : 512 * gr + 512, :]).astype(BF)

    def d_send_p(q):
        @pl.when(is_r)
        def _():
            both(lambda h: d_p["same", h, q].start())

        @pl.when(not_r)
        def _():
            both(lambda h: d_p["other", h, q].start())

    def d_send_core(q):
        @pl.when(is_r)
        def _():
            both(lambda h: d_own[h, q].start())

        @pl.when(not_r)
        def _():
            both(lambda h: d_core[h, q].start())

    def d_recv(q):
        @pl.when(is_r)
        def _():
            both(lambda h: d_own[h, q].wait())
            both(lambda h: d_core[1 - h, q].wait_recv())

        @pl.when(not_r)
        def _():
            def arrive(h):
                d_p["same", h, q].wait_recv()
                d_p["other", 1 - h, q].wait_recv()

            both(arrive)

    def d_sent():
        for q in (0, 1):
            @pl.when(is_r)
            def _():
                both(lambda h: d_p["same", h, q].wait_send())

            @pl.when(not_r)
            def _():
                both(lambda h: d_p["other", h, q].wait_send())
                both(lambda h: d_core[h, q].wait_send())

    q_b.wait_recv()
    for d in (1, -1):
        start(fb_q[d, 1])
    ag_a(1)
    cot_forward(0)

    @pl.when(is_r)
    def _():
        both(lambda h: hid_own[h].wait())
        own_w.wait()

    @pl.when(not_r)
    def _():
        both(lambda h: hid_core[h].wait_recv())

    turn(0)
    ag_b(1, fb_own)
    cot_partner()
    ag_b(1, fb_q)
    cot_rest(0)
    cot_last(0)
    ag_a(2)
    cot_forward(1)
    ag_b(2, fb_own)
    ag_b(2, fb_q)
    cot_rest(1)
    ag_a(3)
    cot_last(1)
    ag_b(3, fb_own)
    cot_end(0)
    cot_end(1)
    own_c.wait()
    both(lambda h: hid_p[h, 0].wait_recv())
    wgrad(1 - vb)
    rs_begin(1)
    ag_a(4)
    ag_b(3, fb_q)
    for k in ORDER[1:]:
        start(ga[k])
    both(lambda h: hid_p[h, 1].wait_recv())
    wgrad(vb)
    rs_begin(0)
    ag_b(4, fb_own)
    unpack(vb)
    dhidden(1, 0)
    d_send_p(0)
    rs_b(1, 2)
    ag_b(4, fb_q)
    rs_first()
    turn(1)
    for k in (0, 1, -1, 2, -2, 3, -3):
        q_a[k].wait_recv()
    for d in (1, -1):
        q_a[4, d].wait_recv()
    unpack(1 - vb)
    layer(1, 0, 0)
    layer(1, 0, 1)
    rs_b(0, 2)
    dhidden(1, 1)
    d_send_p(1)
    rs_a(2, 1)
    layer_core(1, 0)
    layer(1, 1, 0)
    rs_b(1, 3)
    layer(1, 1, 1)
    rs_a(2, -1)
    dhidden(0, 0)
    d_send_core(0)
    layer_core(1, 1)
    rs_b(0, 3)
    layer_y(1, 0)
    dhidden(0, 1)
    d_send_core(1)
    rs_a(3, 1)
    layer(0, 0, 0)
    rs_b(1, 4)
    layer(0, 0, 1)
    rs_a(3, -1)
    layer_y(1, 1)
    layer(0, 1, 0)
    rs_b(0, 4)
    layer(0, 1, 1)
    layer_core(0, 0)
    rs_a(4, 1)
    layer_end(1, 0)
    rs_b_other()
    rs_a(4, -1)
    layer_core(0, 1)
    layer_y(0, 0)
    layer_end(1, 1)
    rs_x(0)
    rs_b_end()
    layer_y(0, 1)
    rs_a_end()
    for q in (0, 1):
        d_recv(q)
    layer_end(0, 0)
    layer_end(0, 1)
    rs_end()

    for cp in sent:
        cp.wait_send()

    @pl.when(not_r)
    def _():
        for cp in swap_w:
            cp.wait_send()
        for o in (0, 1):
            for h in (0, 1):
                hid_p[h, o].wait_send()

    @pl.when(is_r)
    def _():
        both(lambda h: hid_core[1 - h].wait_send())

    d_sent()


def last_kernel(dr, gate, up, out, res, gg_hbm, ug_hbm, lo_hbm, wg_hbm, gg, ug, wg, osem):
    def part(i):
        return pl.ds(PART * i, PART)

    n = UNITS // PART
    saves = [pltpu.make_async_copy(out, lo_hbm, osem.at[2 * n])]
    saves[0].start()
    for p in range(20):
        cols = slice(128 * p, 128 * p + 128)
        wg[0:48, cols] = res[48 * p : 48 * p + 48, :] * SCALE
        wg[48:50, cols] = res[960 + 2 * p : 962 + 2 * p, :] * SCALE
    saves.append(pltpu.make_async_copy(wg, wg_hbm, osem.at[2 * n + 1]))
    saves[1].start()
    for i in range(n):
        @pl.loop(0, PART // 16)
        def _(k):
            r = pl.ds(pl.multiple_of(PART * i + 16 * k, 16), 16)
            dv = dr[r, :].astype(F32)
            gv = gate[r, :].astype(F32)
            uv = up[r, :].astype(F32)
            sv = jax.nn.sigmoid(gv)
            gg[r, :] = (dv * uv * sv * (1.0 + gv * (1.0 - sv))).astype(BF)
            ug[r, :] = (dv * (gv * sv)).astype(BF)

        for j, (src, dst) in enumerate(((gg, gg_hbm), (ug, ug_hbm))):
            cp = pltpu.make_async_copy(src.at[part(i)], dst.at[part(i)], osem.at[2 * i + j])
            cp.start()
            saves.append(cp)
    for cp in saves:
        cp.wait()


def body(gate_pre, up_pre, down_codes, down_scales, cotangent):
    vmem = pl.BlockSpec(memory_space=pltpu.VMEM)
    anywhere = pl.BlockSpec(memory_space=pl.ANY)
    gate_t, up_t = gate_pre.T, up_pre.T
    out, dhid, total = pl.pallas_call(
        kernel,
        out_shape=(
            jax.ShapeDtypeStruct((64, D), BF),
            jax.ShapeDtypeStruct((UNITS, TOK), BF),
            jax.ShapeDtypeStruct((WR, 128), F32),
        ),
        in_specs=[anywhere, anywhere, anywhere, vmem, anywhere],
        out_specs=(vmem,) * 3,
        scratch_shapes=[
            pltpu.VMEM((UNITS, TOK), BF),
            pltpu.VMEM((UNITS, TOK), BF),
            pltpu.VMEM((50, D), BF),
            pltpu.VMEM((64, D), BF),
            pltpu.VMEM((16, WR, 128), BF),
            pltpu.VMEM((WR, 128), BF),
            pltpu.VMEM((HALF, D), BF),
            pltpu.VMEM((1024, D), BF),
            pltpu.VMEM((UNITS, TOK), BF),
            pltpu.VMEM((HALF, 1024), BF),
            pltpu.VMEM((1024, HALF), BF),
            pltpu.VMEM((TOK, TOK), BF),
            pltpu.VMEM((16, WR, 128), BF),
            pltpu.VMEM((8, AG, 128), BF),
            pltpu.VMEM((2, 4, AG, 128), BF),
            pltpu.VMEM((2, 2, 4, BG, 128), BF),
            pltpu.VMEM((BG, 128), BF),
            pltpu.VMEM((BG, 128), BF),
            pltpu.VMEM((WR, 128), BF),
            pltpu.VMEM((WR, 128), BF),
            pltpu.VMEM((2, 2, 2, 256, 1280), BF),
            pltpu.VMEM((2, 2, 256, 1280), BF),
            pltpu.VMEM((2, 2, 2, 32, 1280), BF),
            pltpu.VMEM((2, 2, 2, 64, 1280), BF),
            pltpu.VMEM((2, 64, 1280), BF),
            pltpu.VMEM((2, 64, 1280), BF),
            pltpu.VMEM((2, HALF, TOK), BF),
            pltpu.SemaphoreType.DMA((NSEM,)),
            pltpu.SemaphoreType.DMA((NSEM,)),
            pltpu.SemaphoreType.DMA((16,)),
        ],
        compiler_params=pltpu.CompilerParams(
            collective_id=0, has_side_effects=True, vmem_limit_bytes=LIMIT
        ),
        cost_estimate=pl.CostEstimate(flops=25_000_000_000, bytes_accessed=10_000_000, transcendentals=2_000_000),
    )(gate_t, up_t, down_codes, down_scales.T, cotangent)

    gate_grad, up_grad, layer_out, weight_grad = pl.pallas_call(
        last_kernel,
        out_shape=(
            jax.ShapeDtypeStruct((UNITS, TOK), BF),
            jax.ShapeDtypeStruct((UNITS, TOK), BF),
            jax.ShapeDtypeStruct((64, D), BF),
            jax.ShapeDtypeStruct((50, D), F32),
        ),
        in_specs=[vmem] * 5,
        out_specs=(anywhere,) * 4,
        scratch_shapes=[
            pltpu.VMEM((UNITS, TOK), BF),
            pltpu.VMEM((UNITS, TOK), BF),
            pltpu.VMEM((50, D), F32),
            pltpu.SemaphoreType.DMA((2 * UNITS // PART + 2,)),
        ],
        compiler_params=pltpu.CompilerParams(vmem_limit_bytes=24 << 20),
        cost_estimate=pl.CostEstimate(flops=20_000_000, bytes_accessed=10_000_000, transcendentals=1_000_000),
    )(dhid, gate_t, up_t, out, total)
    return layer_out, gate_grad.T, up_grad.T, weight_grad


def solution(mesh):
    return jax.shard_map(
        body,
        mesh=mesh,
        in_specs=(
            P("dp", "tensor"),
            P("dp", "tensor"),
            P(("tensor", "dp"), None),
            P(("tensor", "dp"), None),
            P(("dp", "tensor"), None),
        ),
        out_specs=(
            P(("dp", "tensor"), None),
            P("dp", "tensor"),
            P("dp", "tensor"),
            P(("tensor", "dp"), None),
        ),
        check_vma=False,
    )
```

```python
import jax
import jax.numpy as jnp
from jax import lax
from jax.experimental import pallas as pl
from jax.experimental.pallas import tpu as pltpu
from jax.sharding import PartitionSpec as P

MESH = pl.DeviceIdType.MESH
BF = jnp.bfloat16
F32 = jnp.float32
D = 2560
TOK = 512
UNITS = 1600
HALF = 800
WR = 1008
AR, BR = 576, 432
AG, BG = 480, 528
NSEM = 160
LIMIT = 400 << 17
PART = 160
SCALE = float(16384) ** -0.5
ORDER = (4, 3, -3, 2, -2, 1, -1, 0)


def dot(a, b):
    return jnp.dot(a, b, preferred_element_type=F32)


def dot_nt(a, b):
    return lax.dot_general(a, b, (((1,), (1,)), ((), ())), preferred_element_type=F32)


def kernel(
    gate_hbm, up_hbm, codes_hbm, scales_ref, cot_hbm,
    out_ref, dr, res,
    gate, up, codes_ref, cot_in, wire, stage, w, cot, hid, ht, hs, eye, g, x_in, ra, rb, fq, fb, stage2, stage3,
    lp, lc, ly, lf, lz, lq, dd, ssem, rsem, lsem,
):
    dp, t = lax.axis_index("dp"), lax.axis_index("tensor")
    x, z, y, c = dp // 8, dp % 8, t // 2, t % 2
    half = x // 2
    xb = x % 2
    is_r = c == half
    not_r = c != half
    vb = jnp.where(is_r, xb, 1 - xb)
    zdev = {1: (8 * x + (z + 1) % 8, t), -1: (8 * x + (z + 7) % 8, t)}
    ydev = {1: (dp, 2 * ((y + 1) % 4) + c), -1: (dp, 2 * ((y + 3) % 4) + c)}
    core = (dp, 2 * y + 1 - c)
    qdev = (8 * (x + 1 - 2 * xb) + z, t)
    pdp = 8 * (3 - x) + z
    psame = (pdp, t)
    pother = (pdp, 2 * y + 1 - c)
    pcore = ((pdp, 2 * y), (pdp, 2 * y + 1))

    count = [0]
    index = {}

    def rc(src, dst, dev):
        i = count[0]
        count[0] += 1
        cp = pltpu.make_async_remote_copy(
            src_ref=src, dst_ref=dst, send_sem=ssem.at[i], recv_sem=rsem.at[i],
            device_id=dev, device_id_type=MESH,
        )
        index[id(cp)] = i
        return cp

    sent = []

    def start(cp):
        cp.start()
        sent.append(cp)

    load_gate = pltpu.make_async_copy(gate_hbm, gate, lsem.at[0])
    load_up = pltpu.make_async_copy(up_hbm, up, lsem.at[1])
    load_codes = pltpu.make_async_copy(codes_hbm, codes_ref, lsem.at[7])
    load_cot = pltpu.make_async_copy(cot_hbm, cot_in, lsem.at[8])
    load_codes.start()
    load_cot.start()
    load_gate.start()
    load_up.start()

    barrier = pltpu.get_barrier_semaphore()
    everyone = (zdev[1], zdev[-1], ydev[1], ydev[-1], core, qdev, psame, pother)
    for dev in everyone:
        pl.semaphore_signal(barrier, inc=1, device_id=dev, device_id_type=MESH)

    left = []
    scales = scales_ref[...].T
    load_codes.wait()
    for p in range(20):
        scale = scales[:, p // 2 : p // 2 + 1]
        piece = codes_ref[:, 128 * p : 128 * p + 128].astype(F32) * scale
        stage[48 * p : 48 * p + 48, :] = piece[:48].astype(BF)
        left.append(piece[48:50])
    left.append(jnp.zeros((8, 128), F32))
    stage[960:1008, :] = jnp.concatenate(left, axis=0).astype(BF)

    load_cot.wait()
    pl.semaphore_wait(barrier, len(everyone))

    def blk(b, k):
        return 8 * b + lax.rem(z + k + 8, 8)

    rows_a = slice(0, AR)
    rows_b = slice(AR, WR)
    half_a = {1: pl.ds(0, 288), -1: pl.ds(288, 288)}
    half_b = {1: pl.ds(AR, 224), -1: pl.ds(AR + 224, 208)}
    own_slot = 8 * vb + z

    swap_w = [rc(stage.at[rows], wire.at[8 * xb + z, rows], pother) for rows in (rows_b, rows_a)]
    own_w = pltpu.make_async_copy(stage, wire.at[own_slot], lsem.at[2])

    def ring(b, rows, halves):
        return {
            (d, s): rc(
                wire.at[blk(b, -d * (s - 1)), rows if s < 4 else halves[d]],
                wire.at[blk(b, -d * (s - 1)), rows if s < 4 else halves[d]],
                zdev[d],
            )
            for s in (1, 2, 3, 4)
            for d in (1, -1)
        }

    fa = ring(vb, rows_a, half_a)
    fb_own = ring(vb, rows_b, half_b)
    fb_q = ring(1 - vb, rows_b, half_b)
    q_b = rc(wire.at[own_slot, rows_b], wire.at[own_slot, rows_b], qdev)
    q_a = {
        k: rc(wire.at[blk(vb, k), rows_a], wire.at[blk(vb, k), rows_a], qdev)
        for k in (0, 1, -1, 2, -2, 3, -3)
    }
    for d in (1, -1):
        q_a[4, d] = rc(wire.at[blk(vb, 4), half_a[d]], wire.at[blk(vb, 4), half_a[d]], qdev)

    begin_b = (q_b, fb_own[1, 1], fb_own[-1, 1])
    begin_a = (fa[1, 1], fa[-1, 1], q_a[0])

    def from_stage(cp, rows, dev):
        i = index[id(cp)]
        pltpu.make_async_remote_copy(
            src_ref=stage.at[rows], dst_ref=wire.at[own_slot, rows], send_sem=ssem.at[i], recv_sem=rsem.at[i],
            device_id=dev, device_id_type=MESH,
        ).start()

    sent.extend((q_b, fa[1, 1], fa[-1, 1], fb_own[1, 1], fb_own[-1, 1], q_a[0]))

    def ag_a(s):
        for d in (1, -1):
            fa[d, s].wait_recv()
            if s < 4:
                start(fa[d, s + 1])
                start(q_a[-d * s])
            else:
                start(q_a[4, d])

    def ag_b(s, which):
        for d in (1, -1):
            which[d, s].wait_recv()
            if s < 4:
                start(which[d, s + 1])

    def crow(gr, tt):
        return pl.multiple_of(512 * gr + 64 * tt, 32)

    def cblk(gr, yy, off=0, n=64):
        return cot.at[pl.ds(pl.multiple_of(512 * gr + 64 * (2 * yy + c) + off, 32), n)]

    y1, ym1, y2 = (y + 1) % 4, (y + 3) % 4, (y + 2) % 4
    cot_p = {
        o: rc(cot_in.at[pl.ds(o, 32)], cblk(1, y, o, 32), psame) for o in (0, 32)
    }
    own_c = pltpu.make_async_copy(cot_in, cblk(0, y), lsem.at[3])
    cot_y, cot_h, cot_core = {}, {}, {}
    first = {1: 0, -1: 32}
    for gr in (0, 1):
        for d in (1, -1):
            for o in (0, 32):
                mine = cot_in.at[pl.ds(o, 32)] if gr == 0 else cblk(1, y, o, 32)
                cot_y[gr, d, o] = rc(mine, cblk(gr, y, o, 32), ydev[d])
        cot_h[gr, 1] = rc(cblk(gr, ym1, 0, 32), cblk(gr, ym1, 0, 32), ydev[1])
        cot_h[gr, -1] = rc(cblk(gr, y1, 32, 32), cblk(gr, y1, 32, 32), ydev[-1])
        mine = cot_in if gr == 0 else cblk(1, y)
        cot_core[gr, 0] = rc(mine, cblk(gr, y), core)
        cot_core[gr, 1] = rc(cblk(gr, ym1), cblk(gr, ym1), core)
        cot_core[gr, -1] = rc(cblk(gr, y1), cblk(gr, y1), core)
        cot_core[gr, 2] = rc(cblk(gr, y2, 0, 32), cblk(gr, y2, 0, 32), core)
        cot_core[gr, -2] = rc(cblk(gr, y2, 32, 32), cblk(gr, y2, 32, 32), core)

    def cot_begin():
        for o in (0, 1):
            for d in (1, -1):
                start(cot_y[0, d, first[d] if o == 0 else 32 - first[d]])
        start(cot_core[0, 0])

    def cot_partner():
        for o in (0, 32):
            cot_p[o].wait_recv()
        for o in (0, 1):
            for d in (1, -1):
                start(cot_y[1, d, first[d] if o == 0 else 32 - first[d]])
        start(cot_core[1, 0])

    def cot_forward(gr):
        for d in (1, -1):
            cot_y[gr, d, first[d]].wait_recv()
            start(cot_h[gr, d])

    def cot_rest(gr):
        for d in (1, -1):
            cot_y[gr, d, 32 - first[d]].wait_recv()
            start(cot_core[gr, d])

    def cot_last(gr):
        for d in (1, -1):
            cot_h[gr, d].wait_recv()
            start(cot_core[gr, 2 * d])

    def cot_end(gr):
        for k in (0, 1, -1, 2, -2):
            cot_core[gr, k].wait_recv()

    def rows_of(h, b):
        return pl.ds(pl.multiple_of(HALF * h + 400 * b, 16), 400)

    def cols_of(gr):
        return slice(512 * gr, 512 * gr + 512)

    hid_p, hid_core, hid_own = {}, {}, {}
    for h in (0, 1):
        v_to = jnp.where(h == 1 - half, 1 - xb, xb)
        for o in (0, 1):
            b = 1 - v_to if o == 0 else v_to
            hid_p[h, o] = rc(hid.at[rows_of(h, b)], ht.at[rows_of(0, b), cols_of(1)], pcore[h])
    for h in (0, 1):
        whole = hid.at[HALF * h : HALF * h + HALF]
        hid_core[h] = rc(whole, ht.at[:, cols_of(0)], core)
        hid_own[h] = pltpu.make_async_copy(whole, ht.at[:, cols_of(0)], lsem.at[4])

    def hidden_rows(lo, hi):
        @pl.loop(lo, hi)
        def _(i):
            r = pl.ds(pl.multiple_of(32 * i, 32), 32)
            gv = gate[r, :].astype(F32)
            uv = up[r, :].astype(F32)
            hid[r, :] = (gv * jax.nn.sigmoid(gv) * uv).astype(BF)

    def both(fn):
        for h in (0, 1):
            pl.when(c == h)(lambda h=h: fn(h))

    def cot_to_partner():
        for o in (0, 32):
            cot_p[o].start()

    sent.extend(cot_p.values())

    @pl.when(not_r)
    def _():
        for cp in swap_w:
            cp.start()
        cot_to_partner()

    own_c.start()
    cot_begin()

    @pl.when(is_r)
    def _():
        from_stage(q_b, rows_b, qdev)
        for d in (1, -1):
            from_stage(fa[d, 1], rows_a, zdev[d])
        for d in (1, -1):
            from_stage(fb_own[d, 1], rows_b, zdev[d])
        from_stage(q_a[0], rows_a, qdev)
        own_w.start()

    row = lax.broadcasted_iota(jnp.int32, (TOK, TOK), 0)
    lane = lax.broadcasted_iota(jnp.int32, (TOK, TOK), 1)
    eye[...] = jnp.where(row == lane, 1.0, 0.0).astype(BF)

    load_gate.wait()
    load_up.wait()
    hidden_rows(0, 15)

    pl.when(is_r)(cot_to_partner)

    @pl.when(not_r)
    def _():
        for cp, begin in zip(swap_w, (begin_b, begin_a)):
            cp.wait_recv()
            for follow in begin:
                follow.start()

    hidden_rows(15, 50)

    @pl.when(not_r)
    def _():
        for o in (0, 1):
            for h in (0, 1):
                hid_p[h, o].start()

    @pl.when(is_r)
    def _():
        both(lambda h: hid_own[h].start())
        both(lambda h: hid_core[1 - h].start())

    def turn(gr):
        hs[512 * gr : 512 * gr + 512, :] = dot_nt(eye[...], ht[:, cols_of(gr)]).astype(BF)

    def wgrad(b):
        left = [[] for _ in range(8)]
        lhs = ht[pl.ds(pl.multiple_of(400 * b, 16), 400), :]
        for n in range(5):
            acc = dot(lhs, cot[:, 512 * n : 512 * n + 512])
            for i in range(8):
                for j in range(4):
                    p = 4 * n + j
                    col = acc[50 * i : 50 * i + 50, 128 * j : 128 * j + 128]
                    g[8 * b + i, 48 * p : 48 * p + 48, :] = col[:48].astype(BF)
                    left[i].append(col[48:50])
        for i in range(8):
            tail = jnp.concatenate(left[i] + [jnp.zeros((8, 128), F32)], axis=0)
            g[8 * b + i, 960:1008, :] = tail.astype(BF)

    def unpack(b):
        tails = [wire[8 * b + i, 960:1008, :].astype(F32) for i in range(8)]
        for p in range(20):
            rows = []
            for i in range(8):
                rows.append(wire[8 * b + i, 48 * p : 48 * p + 48, :].astype(F32))
                rows.append(tails[i][2 * p : 2 * p + 2])
            w[pl.ds(pl.multiple_of(400 * b, 16), 400), 128 * p : 128 * p + 128] = jnp.concatenate(rows, axis=0).astype(BF)

    cut_a, cut_b = slice(0, AG), slice(AG, WR)
    part_b = {1: pl.ds(AG, 272), -1: pl.ds(AG + 272, 256)}

    def kidx(k):
        return k + 3

    ga = {k: rc(g.at[blk(1 - vb, k), cut_a], x_in.at[kidx(k)], qdev) for k in ORDER}
    ha = {1: pl.ds(0, 240), -1: pl.ds(240, 240)}
    hb = {1: pl.ds(0, 272), -1: pl.ds(272, 256)}
    ra_c, rb_c = {}, {}
    for s in (1, 2, 3, 4):
        for d in (1, -1):
            if s == 1:
                ra_c[d, s] = rc(x_in.at[kidx(4), ha[d]], ra.at[(1 - d) // 2, 0, ha[d]], zdev[d])
            else:
                ra_c[d, s] = rc(x_in.at[kidx(d * (5 - s))], ra.at[(1 - d) // 2, s - 1], zdev[d])
            for bb, b in ((0, vb), (1, 1 - vb)):
                if s == 1:
                    rb_c[bb, d, s] = rc(g.at[blk(b, 4), part_b[d]], rb.at[bb, (1 - d) // 2, 0, hb[d]], zdev[d])
                else:
                    rb_c[bb, d, s] = rc(g.at[blk(b, d * (5 - s)), cut_b], rb.at[bb, (1 - d) // 2, s - 1], zdev[d])
    fin_q = rc(fq, fb, qdev)
    swap_ga = rc(stage2.at[cut_a], stage3.at[cut_a], pother)
    swap_gb = rc(stage2.at[cut_b], stage3.at[cut_b], pother)

    def add_into(dst, *terms):
        n = dst.shape[0]
        step = next(v for v in (176, 160, 136, 128, 120, 32, 16) if n % v == 0 and v % 16 == 0)

        @pl.loop(0, n // step)
        def _(i):
            r = pl.ds(pl.multiple_of(i * step, 16), step)
            v = dst[r, :].astype(F32)
            for term in terms:
                v = v + term[r, :].astype(F32)
            dst[r, :] = v.astype(dst.dtype)

    def rs_begin(bb):
        for d in (1, -1):
            start(rb_c[bb, d, 1])
        if bb == 1:
            start(ga[4])

    def rs_x(k):
        ga[k].wait_recv()
        add_into(x_in.at[kidx(k)], g.at[blk(vb, k), cut_a])

    def rs_first():
        rs_x(4)
        for d in (1, -1):
            start(ra_c[d, 1])

    def rs_a(s, d):
        k = d * (5 - s)
        rs_x(k)
        ra_c[d, s - 1].wait_recv()
        rows = ha[d] if s == 2 else pl.ds(0, AG)
        add_into(x_in.at[kidx(k), rows], ra.at[(1 - d) // 2, s - 2, rows])
        start(ra_c[d, s])

    def rs_b(bb, s):
        b = 1 - vb if bb == 1 else vb
        for d in (1, -1):
            k = d * (5 - s)
            rb_c[bb, d, s - 1].wait_recv()
            if s == 2:
                dst, src = g.at[blk(b, k), part_b[d]], rb.at[bb, (1 - d) // 2, 0, hb[d]]
            else:
                dst, src = g.at[blk(b, k), cut_b], rb.at[bb, (1 - d) // 2, s - 2]
            add_into(dst, src)
            start(rb_c[bb, d, s])

    def rs_b_other():
        for d in (1, -1):
            rb_c[1, d, 4].wait_recv()
        fq[...] = (
            g[blk(1 - vb, 0), cut_b, :].astype(F32)
            + rb[1, 0, 3].astype(F32)
            + rb[1, 1, 3].astype(F32)
        ).astype(BF)
        start(fin_q)

    def swap_out(rows, cp, total):
        res[rows, :] = total

        @pl.when(not_r)
        def _():
            stage2[rows, :] = total.astype(BF)
            cp.start()

    def rs_b_end():
        for d in (1, -1):
            rb_c[0, d, 4].wait_recv()
        part = g[blk(vb, 0), cut_b, :].astype(F32) + rb[0, 0, 3].astype(F32) + rb[0, 1, 3].astype(F32)
        fin_q.wait_recv()
        swap_out(cut_b, swap_gb, part + fb[...].astype(F32))

    def rs_a_end():
        for d in (1, -1):
            ra_c[d, 4].wait_recv()
        total = x_in[kidx(0)].astype(F32) + ra[0, 3].astype(F32) + ra[1, 3].astype(F32)
        swap_out(cut_a, swap_ga, total)

    def rs_end():
        @pl.when(not_r)
        def _():
            swap_gb.wait_recv()
            res[cut_b, :] = stage3[cut_b, :].astype(F32)
            swap_ga.wait_recv()
            res[cut_a, :] = stage3[cut_a, :].astype(F32)
            swap_ga.wait_send()
            swap_gb.wait_send()

    def layer(gr, ch, n):
        off = 640 * n
        acc = dot(hs[512 * gr : 512 * gr + 512, :], w[:, 1280 * ch + off : 1280 * ch + off + 640])
        for tt in range(8):
            r = 64 * (tt // 2)
            lp[gr, ch, tt % 2, r : r + 64, off : off + 640] = acc[64 * tt : 64 * tt + 64].astype(BF)
        if n == 1:
            start(l_core[gr, ch])

    l_core, l_y1, l_y2, l_p = {}, {}, {}, {}

    def yrow(yy, off=0, n=64):
        return pl.ds(pl.multiple_of(64 * yy + off, 32), n)

    for gr in (1, 0):
        for ch in (0, 1):
            l_core[gr, ch] = rc(lp.at[gr, ch, 1 - c], lc.at[gr, ch], core)
            for d in (1, -1):
                o = 0 if d == 1 else 32
                l_y1[gr, ch, d] = rc(lc.at[gr, ch, yrow(y2, o, 32)], ly.at[gr, ch, (1 - d) // 2], ydev[d])
                to = y1 if d == 1 else ym1
                l_y2[gr, ch, d] = rc(lc.at[gr, ch, yrow(to)], lf.at[gr, ch, (1 - d) // 2], ydev[d])
    for ch in (0, 1):
        l_p[ch] = rc(lz.at[ch], lq.at[ch], psame)

    def layer_core(gr, ch):
        l_core[gr, ch].wait_recv()
        add_into(lc.at[gr, ch], lp.at[gr, ch, c])
        for d in (1, -1):
            start(l_y1[gr, ch, d])

    def layer_y(gr, ch):
        for d in (1, -1):
            l_y1[gr, ch, d].wait_recv()
            o = 0 if d == 1 else 32
            to = y1 if d == 1 else ym1
            add_into(lc.at[gr, ch, yrow(to, o, 32)], ly.at[gr, ch, (1 - d) // 2])
            start(l_y2[gr, ch, d])

    def layer_end(gr, ch):
        for d in (1, -1):
            l_y2[gr, ch, d].wait_recv()
        total = lc[gr, ch, yrow(y), :].astype(F32) + lf[gr, ch, 0].astype(F32) + lf[gr, ch, 1].astype(F32)
        if gr == 1:
            lz[ch] = total.astype(BF)
            start(l_p[ch])
        else:
            l_p[ch].wait_recv()
            out_ref[:, 1280 * ch : 1280 * ch + 1280] = (total + lq[ch].astype(F32)).astype(BF)

    def half_of(o):
        return vb if o == 0 else 1 - vb

    def rows_at(q):
        return pl.ds(pl.multiple_of(400 * q, 16), 400)

    def drows(h, o):
        return pl.ds(pl.multiple_of(HALF * h + 400 * half_of(o), 16), 400)

    d_p, d_core, d_own = {}, {}, {}
    for h in (0, 1):
        for q in (0, 1):
            src = dd.at[1, rows_at(half_of(q))]
            d_p["same", h, q] = rc(src, dr.at[drows(h, q)], psame)
            d_p["other", h, q] = rc(src, dr.at[drows(h, q)], pother)
            src = dd.at[0, rows_at(half_of(q))]
            d_core[h, q] = rc(src, dr.at[drows(h, q)], core)
            d_own[h, q] = pltpu.make_async_copy(src, dr.at[drows(h, q)], lsem.at[5 + q])

    def dhidden(gr, o, k):
        r = rows_at(half_of(o))
        lo = 256 * k
        dd[gr, r, lo : lo + 256] = dot_nt(w[r, :], cot[512 * gr + lo : 512 * gr + lo + 256, :]).astype(BF)

    def d_send_p(q):
        @pl.when(is_r)
        def _():
            both(lambda h: d_p["same", h, q].start())

        @pl.when(not_r)
        def _():
            both(lambda h: d_p["other", h, q].start())

    def d_send_core(q):
        @pl.when(is_r)
        def _():
            both(lambda h: d_own[h, q].start())

        @pl.when(not_r)
        def _():
            both(lambda h: d_core[h, q].start())

    def d_recv(q):
        @pl.when(is_r)
        def _():
            both(lambda h: d_own[h, q].wait())
            both(lambda h: d_core[1 - h, q].wait_recv())

        @pl.when(not_r)
        def _():
            def arrive(h):
                d_p["same", h, q].wait_recv()
                d_p["other", 1 - h, q].wait_recv()

            both(arrive)

    def d_sent():
        for q in (0, 1):
            @pl.when(is_r)
            def _():
                both(lambda h: d_p["same", h, q].wait_send())

            @pl.when(not_r)
            def _():
                both(lambda h: d_p["other", h, q].wait_send())
                both(lambda h: d_core[h, q].wait_send())

    q_b.wait_recv()
    for d in (1, -1):
        start(fb_q[d, 1])
    ag_a(1)
    cot_forward(0)

    @pl.when(is_r)
    def _():
        both(lambda h: hid_own[h].wait())
        own_w.wait()

    @pl.when(not_r)
    def _():
        both(lambda h: hid_core[h].wait_recv())

    turn(0)
    ag_b(1, fb_own)
    cot_partner()
    ag_b(1, fb_q)
    cot_rest(0)
    cot_last(0)
    ag_a(2)
    cot_forward(1)
    ag_b(2, fb_own)
    ag_b(2, fb_q)
    cot_rest(1)
    ag_a(3)
    cot_last(1)
    ag_b(3, fb_own)
    cot_end(0)
    cot_end(1)
    own_c.wait()
    both(lambda h: hid_p[h, 0].wait_recv())
    wgrad(1 - vb)
    rs_begin(1)
    ag_a(4)
    ag_b(3, fb_q)
    for k in ORDER[1:]:
        start(ga[k])
    both(lambda h: hid_p[h, 1].wait_recv())
    wgrad(vb)
    rs_begin(0)
    ag_b(4, fb_own)
    unpack(vb)
    dhidden(1, 0, 0)
    dhidden(1, 0, 1)
    d_send_p(0)
    rs_b(1, 2)
    ag_b(4, fb_q)
    rs_first()
    turn(1)
    for k in (0, 1, -1, 2, -2, 3, -3):
        q_a[k].wait_recv()
    for d in (1, -1):
        q_a[4, d].wait_recv()
    unpack(1 - vb)
    layer(1, 0, 0)
    layer(1, 0, 1)
    rs_b(0, 2)
    dhidden(1, 1, 0)
    rs_a(2, 1)
    dhidden(1, 1, 1)
    d_send_p(1)
    layer_core(1, 0)
    layer(1, 1, 0)
    rs_b(1, 3)
    layer(1, 1, 1)
    rs_a(2, -1)
    dhidden(0, 0, 0)
    layer_core(1, 1)
    rs_b(0, 3)
    dhidden(0, 0, 1)
    d_send_core(0)
    layer_y(1, 0)
    dhidden(0, 1, 0)
    rs_a(3, 1)
    dhidden(0, 1, 1)
    d_send_core(1)
    layer(0, 0, 0)
    rs_b(1, 4)
    layer(0, 0, 1)
    rs_a(3, -1)
    layer_y(1, 1)
    layer(0, 1, 0)
    rs_b(0, 4)
    layer(0, 1, 1)
    layer_core(0, 0)
    rs_a(4, 1)
    layer_end(1, 0)
    rs_b_other()
    rs_a(4, -1)
    layer_core(0, 1)
    layer_y(0, 0)
    layer_end(1, 1)
    rs_x(0)
    rs_b_end()
    layer_y(0, 1)
    rs_a_end()
    for q in (0, 1):
        d_recv(q)
    layer_end(0, 0)
    layer_end(0, 1)
    rs_end()

    for cp in sent:
        cp.wait_send()

    @pl.when(not_r)
    def _():
        for cp in swap_w:
            cp.wait_send()
        for o in (0, 1):
            for h in (0, 1):
                hid_p[h, o].wait_send()

    @pl.when(is_r)
    def _():
        both(lambda h: hid_core[1 - h].wait_send())

    d_sent()


def last_kernel(dr, gate, up, out, res, gg_hbm, ug_hbm, lo_hbm, wg_hbm, gg, ug, wg, osem):
    def part(i):
        return pl.ds(PART * i, PART)

    n = UNITS // PART
    saves = [pltpu.make_async_copy(out, lo_hbm, osem.at[2 * n])]
    saves[0].start()
    for p in range(20):
        cols = slice(128 * p, 128 * p + 128)
        wg[0:48, cols] = res[48 * p : 48 * p + 48, :] * SCALE
        wg[48:50, cols] = res[960 + 2 * p : 962 + 2 * p, :] * SCALE
    saves.append(pltpu.make_async_copy(wg, wg_hbm, osem.at[2 * n + 1]))
    saves[1].start()
    for i in range(n):
        @pl.loop(0, PART // 16)
        def _(k):
            r = pl.ds(pl.multiple_of(PART * i + 16 * k, 16), 16)
            dv = dr[r, :].astype(F32)
            gv = gate[r, :].astype(F32)
            uv = up[r, :].astype(F32)
            sv = jax.nn.sigmoid(gv)
            gg[r, :] = (dv * uv * sv * (1.0 + gv * (1.0 - sv))).astype(BF)
            ug[r, :] = (dv * (gv * sv)).astype(BF)

        for j, (src, dst) in enumerate(((gg, gg_hbm), (ug, ug_hbm))):
            cp = pltpu.make_async_copy(src.at[part(i)], dst.at[part(i)], osem.at[2 * i + j])
            cp.start()
            saves.append(cp)
    for cp in saves:
        cp.wait()


def body(gate_pre, up_pre, down_codes, down_scales, cotangent):
    vmem = pl.BlockSpec(memory_space=pltpu.VMEM)
    anywhere = pl.BlockSpec(memory_space=pl.ANY)
    gate_t, up_t = gate_pre.T, up_pre.T
    out, dhid, total = pl.pallas_call(
        kernel,
        out_shape=(
            jax.ShapeDtypeStruct((64, D), BF),
            jax.ShapeDtypeStruct((UNITS, TOK), BF),
            jax.ShapeDtypeStruct((WR, 128), F32),
        ),
        in_specs=[anywhere, anywhere, anywhere, vmem, anywhere],
        out_specs=(vmem,) * 3,
        scratch_shapes=[
            pltpu.VMEM((UNITS, TOK), BF),
            pltpu.VMEM((UNITS, TOK), BF),
            pltpu.VMEM((50, D), BF),
            pltpu.VMEM((64, D), BF),
            pltpu.VMEM((16, WR, 128), BF),
            pltpu.VMEM((WR, 128), BF),
            pltpu.VMEM((HALF, D), BF),
            pltpu.VMEM((1024, D), BF),
            pltpu.VMEM((UNITS, TOK), BF),
            pltpu.VMEM((HALF, 1024), BF),
            pltpu.VMEM((1024, HALF), BF),
            pltpu.VMEM((TOK, TOK), BF),
            pltpu.VMEM((16, WR, 128), BF),
            pltpu.VMEM((8, AG, 128), BF),
            pltpu.VMEM((2, 4, AG, 128), BF),
            pltpu.VMEM((2, 2, 4, BG, 128), BF),
            pltpu.VMEM((BG, 128), BF),
            pltpu.VMEM((BG, 128), BF),
            pltpu.VMEM((WR, 128), BF),
            pltpu.VMEM((WR, 128), BF),
            pltpu.VMEM((2, 2, 2, 256, 1280), BF),
            pltpu.VMEM((2, 2, 256, 1280), BF),
            pltpu.VMEM((2, 2, 2, 32, 1280), BF),
            pltpu.VMEM((2, 2, 2, 64, 1280), BF),
            pltpu.VMEM((2, 64, 1280), BF),
            pltpu.VMEM((2, 64, 1280), BF),
            pltpu.VMEM((2, HALF, TOK), BF),
            pltpu.SemaphoreType.DMA((NSEM,)),
            pltpu.SemaphoreType.DMA((NSEM,)),
            pltpu.SemaphoreType.DMA((16,)),
        ],
        compiler_params=pltpu.CompilerParams(
            collective_id=0, has_side_effects=True, vmem_limit_bytes=LIMIT
        ),
        cost_estimate=pl.CostEstimate(flops=25_000_000_000, bytes_accessed=10_000_000, transcendentals=2_000_000),
    )(gate_t, up_t, down_codes, down_scales.T, cotangent)

    gate_grad, up_grad, layer_out, weight_grad = pl.pallas_call(
        last_kernel,
        out_shape=(
            jax.ShapeDtypeStruct((UNITS, TOK), BF),
            jax.ShapeDtypeStruct((UNITS, TOK), BF),
            jax.ShapeDtypeStruct((64, D), BF),
            jax.ShapeDtypeStruct((50, D), F32),
        ),
        in_specs=[vmem] * 5,
        out_specs=(anywhere,) * 4,
        scratch_shapes=[
            pltpu.VMEM((UNITS, TOK), BF),
            pltpu.VMEM((UNITS, TOK), BF),
            pltpu.VMEM((50, D), F32),
            pltpu.SemaphoreType.DMA((2 * UNITS // PART + 2,)),
        ],
        compiler_params=pltpu.CompilerParams(vmem_limit_bytes=24 << 20),
        cost_estimate=pl.CostEstimate(flops=20_000_000, bytes_accessed=10_000_000, transcendentals=1_000_000),
    )(dhid, gate_t, up_t, out, total)
    return layer_out, gate_grad.T, up_grad.T, weight_grad


def solution(mesh):
    return jax.shard_map(
        body,
        mesh=mesh,
        in_specs=(
            P("dp", "tensor"),
            P("dp", "tensor"),
            P(("tensor", "dp"), None),
            P(("tensor", "dp"), None),
            P(("dp", "tensor"), None),
        ),
        out_specs=(
            P(("dp", "tensor"), None),
            P("dp", "tensor"),
            P("dp", "tensor"),
            P(("tensor", "dp"), None),
        ),
        check_vma=False,
    )
```
